512 devices in a mesh: gz: 16 (over z, core), gy: 8 (over y), gx: 4 (over x).
Axes of the slice: x: 4, y: 8, z: 8, core: 2. Of those that a mesh axis runs over, the one named last changes fastest.
Arguments:
- features: bfloat16 [48, 32, 16, 512], P(None, 'gz', 'gy', 'gx'), may hold values from -20 to 20
- segment_ids: int32 [32, 16, 512], P('gz', 'gy', 'gx'), may hold values from 0 to 2047, as said below
- kernel_one: bfloat16 [3, 3, 3, 48, 48], replicated, may hold values from -0.15625 to 0.15625
- bias_one: float32 [48], replicated, may hold values from -3 to 3
- kernel_two: bfloat16 [3, 3, 3, 16, 48], replicated, may hold values from -0.15625 to 0.15625
Outputs:
- grad_features: bfloat16 [48, 32, 16, 512], P(None, 'gz', 'gy', 'gx')
- grad_kernel_one: float32 [3, 3, 3, 48, 48], replicated
- grad_bias_one: float32 [48], replicated
- grad_kernel_two: float32 [3, 3, 3, 16, 48], replicated
The draws below stay inside these ranges and needn't reach their ends.
Inputs may be any that keep to these rules, and one draw needn't show every extreme that they name: `segment_ids`: every id occurs at some voxel.
All inputs are finite; a program needn't handle non-finite values.
Results may differ from the reference program's by a relative error of at most 0.017.
Values may be sent and summed in bfloat16 or wider, within the bound.
No kernel may reach another device: no remote copies, remote signals or barrier semaphores. Data moves between devices by JAX's collectives and lax.ppermute only.
A program may use at most 64 MiB of HBM per device.

```python
import jax
import jax.numpy as jnp
from jax import lax

CHANNELS = 48
EMBED_DIM = 16
DEPTH_DEV = 2
ROWS_DEV = 2
COLS_DEV = 128
BLOB_SIZE = 8
DEPTH = 32
ROWS = 16
COLUMNS = 512
VOXELS = 262144
SEGMENTS = 2048


def segment_field(key):
    key_field = jax.random.fold_in(key, 11)
    key_shift, key_order = jax.random.split(key_field)
    cells_depth = DEPTH // BLOB_SIZE + 1
    cells_rows = ROWS // BLOB_SIZE + 1
    cells_cols = COLUMNS // BLOB_SIZE + 1
    cells_total = cells_depth * cells_rows * cells_cols
    half_blob = BLOB_SIZE // 2
    depth_index = jnp.arange(DEPTH, dtype=jnp.int32)[:, None, None]
    row_index = jnp.arange(ROWS, dtype=jnp.int32)[None, :, None]
    col_index = jnp.arange(COLUMNS, dtype=jnp.int32)[None, None, :]
    cell_depth = (depth_index + half_blob) // BLOB_SIZE
    cell_row = (row_index + half_blob) // BLOB_SIZE
    cell_col = (col_index + half_blob) // BLOB_SIZE
    cell_number = (cell_depth * cells_rows + cell_row) * cells_cols + cell_col
    shifts = jax.random.randint(key_shift, (cells_total,), 0, 4)
    sub_label = (depth_index % 2 * 2 + row_index % 2 + shifts[cell_number]) % 4
    shuffled = jax.random.permutation(key_order, cells_total * 4)
    return (shuffled[cell_number * 4 + sub_label] % SEGMENTS).astype(jnp.int32)


def draw_segment_ids(key, part):
    return segment_field(key)


def draw_features(key, part):
    labels = segment_field(key)
    key_local = jax.random.fold_in(key, 5)
    key_offset, key_noise = jax.random.split(key_local, 2)
    offsets = jnp.clip(jax.random.normal(key_offset, (CHANNELS, SEGMENTS), jnp.float32), -3.0, 3.0)
    noise_field = jnp.clip(jax.random.normal(key_noise, (CHANNELS, DEPTH, ROWS, COLUMNS), jnp.float32), -3.5, 3.5)
    depth_index = jnp.arange(DEPTH, dtype=jnp.int32)[:, None, None]
    row_index = jnp.arange(ROWS, dtype=jnp.int32)[None, :, None]
    col_index = jnp.arange(COLUMNS, dtype=jnp.int32)[None, None, :]
    middle = DEPTH // 2
    heavy = (depth_index >= middle) & (depth_index < middle + DEPTH_DEV) & (row_index < ROWS_DEV) & (col_index < COLS_DEV)
    amplitude = jnp.where(heavy, 3.0, 1.0).astype(jnp.float32)
    return (amplitude[None] * (noise_field + offsets[:, labels])).astype(jnp.bfloat16)


def centred(key, shape, scale, reach, held_as=jnp.bfloat16):
    return jnp.clip(scale * jax.random.normal(key, shape, jnp.float32), -reach, reach).astype(held_as)


def setup_inputs(seed: int = 0) -> dict:
    key_list = jax.random.split(jax.random.key(seed), 6)
    return {
        "features": draw_features(jax.random.fold_in(key_list[5], 71), 0),
        "segment_ids": draw_segment_ids(jax.random.fold_in(key_list[5], 71), 0),
        "kernel_one": centred(key_list[2], (3, 3, 3, CHANNELS, CHANNELS), (27 * CHANNELS) ** -0.5, 0.15625),
        "bias_one": centred(key_list[3], (CHANNELS,), 0.5, 3.0, jnp.float32),
        "kernel_two": centred(key_list[4], (3, 3, 3, EMBED_DIM, CHANNELS), (27 * CHANNELS) ** -0.5, 0.15625),
    }


pull_margin = 4.0
push_margin = 8.0

def correlate(padded, weights, depth_len, rows_len, cols_len):
    accumulated = jnp.zeros((weights.shape[3], depth_len * rows_len * cols_len), jnp.float32)
    for offset_depth in range(3):
        for offset_row in range(3):
            for offset_col in range(3):
                window_slice = padded[:, offset_depth:offset_depth + depth_len, offset_row:offset_row + rows_len, offset_col:offset_col + cols_len].reshape(padded.shape[0], -1)
                accumulated = accumulated + jnp.dot(weights[offset_depth, offset_row, offset_col], window_slice, preferred_element_type=jnp.float32)
    return accumulated

def taps_grad(padded, upstream, depth_len, rows_len, cols_len):
    results = []
    for offset_depth in range(3):
        for offset_row in range(3):
            for offset_col in range(3):
                window_slice = padded[:, offset_depth:offset_depth + depth_len, offset_row:offset_row + rows_len, offset_col:offset_col + cols_len].reshape(padded.shape[0], -1)
                results.append(lax.dot_general(upstream, window_slice, (((1,), (1,)), ((), ())), preferred_element_type=jnp.float32))
    return jnp.stack(results).reshape(3, 3, 3, upstream.shape[0], padded.shape[0])

def flipped(weights):
    return jnp.transpose(weights[::-1, ::-1, ::-1], (0, 1, 2, 4, 3))

def pad_grid(field):
    return jnp.pad(field, ((0, 0), (1, 1), (1, 1), (1, 1)))

def push_block(rows_block, centers):
    difference = rows_block[:, None, :] - centers[None, :, :]
    distance = lax.optimization_barrier(jnp.sum(difference * difference, 2))
    hinge_term = jnp.maximum(push_margin - distance, 0.0)
    return -lax.optimization_barrier(jnp.sum(hinge_term[:, :, None] * difference, 1))

def reference(features, segment_ids, kernel_one, bias_one, kernel_two):
    padded_in = pad_grid(features)
    hidden = jnp.maximum(correlate(padded_in, kernel_one, DEPTH, ROWS, COLUMNS) + bias_one[:, None], 0.0).astype(jnp.bfloat16)
    padded_hidden = pad_grid(hidden.reshape(CHANNELS, DEPTH, ROWS, COLUMNS))
    embedding = correlate(padded_hidden, kernel_two, DEPTH, ROWS, COLUMNS)
    segment_flat = segment_ids.reshape(-1)
    segment_sums = jax.ops.segment_sum(embedding.T, segment_flat, num_segments=SEGMENTS)
    counts = jax.ops.segment_sum(jnp.ones(segment_flat.shape, jnp.float32), segment_flat, num_segments=SEGMENTS)
    centers = segment_sums / counts[:, None]
    blocks = centers.reshape(32, SEGMENTS // 32, EMBED_DIM)
    push_grad = lax.map(lambda rows_block: push_block(rows_block, centers), blocks).reshape(SEGMENTS, EMBED_DIM)
    push_grad = push_grad * (8.0 / (SEGMENTS * (SEGMENTS - 1.0)))
    near_center = centers[segment_flat].T
    near_count = counts[segment_flat]
    offset_vec = embedding - near_center
    hinge_term = jnp.maximum(lax.optimization_barrier(jnp.sum(offset_vec * offset_vec, 0)) - pull_margin, 0.0)
    direct = 4.0 * hinge_term * offset_vec / (SEGMENTS * near_count)
    center_grad = push_grad - jax.ops.segment_sum(direct.T, segment_flat, num_segments=SEGMENTS)
    upstream = (VOXELS * (direct + center_grad[segment_flat].T / near_count)).astype(jnp.bfloat16)
    padded_up = pad_grid(upstream.reshape(EMBED_DIM, DEPTH, ROWS, COLUMNS))
    hidden_grad = jnp.where(hidden > 0, correlate(padded_up, flipped(kernel_two), DEPTH, ROWS, COLUMNS), 0.0).astype(jnp.bfloat16)
    padded_grad = pad_grid(hidden_grad.reshape(CHANNELS, DEPTH, ROWS, COLUMNS))
    grad_features = correlate(padded_grad, flipped(kernel_one), DEPTH, ROWS, COLUMNS).astype(jnp.bfloat16).reshape(CHANNELS, DEPTH, ROWS, COLUMNS)
    grad_one = taps_grad(padded_in, hidden_grad, DEPTH, ROWS, COLUMNS) / VOXELS
    grad_bias = lax.optimization_barrier(jnp.sum(hidden_grad.astype(jnp.float32), 1)) / VOXELS
    grad_two = taps_grad(padded_hidden, upstream, DEPTH, ROWS, COLUMNS) / VOXELS
    return (grad_features, grad_one, grad_bias, grad_two)
```

```python
import jax
import jax.numpy as jnp
from jax import lax
from jax.sharding import PartitionSpec as P

EMBED_DIM = 16
SEG_DEV = 4


pull_margin = 4.0
push_margin = 8.0


def extended(block, sides, width):
    for axis, dim in sides:
        count = lax.axis_size(axis)
        forward = [(i, i + 1) for i in range(count - 1)]
        backward = [(target, source) for source, target in forward]
        low = lax.ppermute(
            lax.slice_in_dim(block, block.shape[dim] - width, None, axis=dim), axis, forward
        )
        high = lax.ppermute(lax.slice_in_dim(block, 0, width, axis=dim), axis, backward)
        block = jnp.concatenate([low, block, high], axis=dim)
    return block


def correlate(padded, weights, depth_len, rows_len, cols_len):
    accumulated = jnp.zeros((weights.shape[3], depth_len * rows_len * cols_len), jnp.float32)
    for offset_depth in range(3):
        for offset_row in range(3):
            for offset_col in range(3):
                window_slice = padded[
                    :,
                    offset_depth : offset_depth + depth_len,
                    offset_row : offset_row + rows_len,
                    offset_col : offset_col + cols_len,
                ].reshape(padded.shape[0], -1)
                accumulated = accumulated + jnp.dot(
                    weights[offset_depth, offset_row, offset_col],
                    window_slice,
                    preferred_element_type=jnp.float32,
                )
    return accumulated


def taps_grad(padded, upstream, depth_len, rows_len, cols_len):
    results = []
    for offset_depth in range(3):
        for offset_row in range(3):
            for offset_col in range(3):
                window_slice = padded[
                    :,
                    offset_depth : offset_depth + depth_len,
                    offset_row : offset_row + rows_len,
                    offset_col : offset_col + cols_len,
                ].reshape(padded.shape[0], -1)
                results.append(
                    lax.dot_general(
                        upstream,
                        window_slice,
                        (((1,), (1,)), ((), ())),
                        preferred_element_type=jnp.float32,
                    )
                )
    return jnp.stack(results).reshape(3, 3, 3, upstream.shape[0], padded.shape[0])


def flipped(weights):
    return jnp.transpose(weights[::-1, ::-1, ::-1], (0, 1, 2, 4, 3))


def push_rows(own_centers, centers, scale):
    difference = own_centers.T[:, :, None] - centers.T[:, None, :]
    distance = jnp.sum(difference * difference, 0)
    hinge_term = jnp.maximum(push_margin - distance, 0.0)
    return -scale * jnp.sum(hinge_term[None, :, :] * difference, 2).T


def total(parts):
    flat = jnp.concatenate([part.reshape(-1) for part in parts])
    groups = lax.axis_size(("gy", "gx"))
    layers = lax.axis_size("gz")
    lines = -(-flat.shape[0] // (groups * 1024)) * 8
    padded = jnp.pad(flat, (0, groups * lines * 128 - flat.shape[0])).reshape(groups, lines, 128)
    chunk = jnp.sum(lax.all_to_all(padded, ("gy", "gx"), 0, 0), 0)
    copies = jnp.broadcast_to(chunk[None], (layers, lines, 128))
    chunk = jnp.sum(lax.all_to_all(copies, "gz", 0, 0), 0)
    copies = jnp.broadcast_to(chunk[None], (groups, lines, 128))
    flat = lax.all_to_all(copies, ("gy", "gx"), 0, 0).reshape(-1)
    results, start = [], 0
    for part in parts:
        results.append(flat[start : start + part.size].reshape(part.shape))
        start += part.size
    return results


def shards(features, segment_ids, kernel_one, bias_one, kernel_two):
    channels_in, depth_len, rows_len, cols_len = features.shape
    cells_here = depth_len * rows_len * cols_len
    device_count = lax.axis_size("gz") * lax.axis_size("gy") * lax.axis_size("gx")
    voxels_total = cells_here * device_count
    segment_count = SEG_DEV * device_count
    padded_in = extended(features, (("gz", 1), ("gy", 2), ("gx", 3)), 1)
    hidden = jnp.maximum(
        correlate(padded_in, kernel_one, depth_len, rows_len, cols_len) + bias_one[:, None], 0.0
    ).astype(jnp.bfloat16)
    hidden = hidden.reshape(channels_in, depth_len, rows_len, cols_len)
    padded_hidden = extended(hidden, (("gz", 1), ("gy", 2), ("gx", 3)), 1)
    embedding = correlate(padded_hidden, kernel_two, depth_len, rows_len, cols_len)
    segment_flat = segment_ids.reshape(-1)
    local_sums = jax.ops.segment_sum(embedding.T, segment_flat, num_segments=segment_count)
    local_counts = jax.ops.segment_sum(
        jnp.ones((cells_here,), jnp.float32), segment_flat, num_segments=segment_count
    )
    first_row = lax.axis_index(("gz", "gy", "gx")) * SEG_DEV
    push_scale = 8.0 / (segment_count * (segment_count - 1.0))
    segment_sums, counts = total([local_sums.T, local_counts])
    segment_sums = segment_sums.T
    centers = segment_sums / counts[:, None]
    own_centers = lax.dynamic_slice_in_dim(centers, first_row, SEG_DEV, 0)
    push_grad = push_rows(own_centers, centers, push_scale)
    near_center = centers[segment_flat].T
    near_count = counts[segment_flat]
    offset_vec = embedding - near_center
    hinge_term = jnp.maximum(jnp.sum(offset_vec * offset_vec, 0) - pull_margin, 0.0)
    direct = 4.0 * hinge_term * offset_vec / (segment_count * near_count)
    local_direct = jax.ops.segment_sum(direct.T, segment_flat, num_segments=segment_count)
    placed = lax.dynamic_update_slice_in_dim(
        jnp.zeros((segment_count, EMBED_DIM), jnp.float32), push_grad, first_row, 0
    )
    center_grad = total([(placed - local_direct).T])[0].T
    upstream = (voxels_total * (direct + center_grad[segment_flat].T / near_count)).astype(
        jnp.bfloat16
    )
    padded_up = extended(
        upstream.reshape(EMBED_DIM, depth_len, rows_len, cols_len),
        (("gz", 1), ("gy", 2), ("gx", 3)),
        1,
    )
    hidden_grad = jnp.where(
        hidden.reshape(channels_in, -1) > 0,
        correlate(padded_up, flipped(kernel_two), depth_len, rows_len, cols_len),
        0.0,
    ).astype(jnp.bfloat16)
    padded_grad = extended(
        hidden_grad.reshape(channels_in, depth_len, rows_len, cols_len),
        (("gz", 1), ("gy", 2), ("gx", 3)),
        1,
    )
    grad_features = (
        correlate(padded_grad, flipped(kernel_one), depth_len, rows_len, cols_len)
        .astype(jnp.bfloat16)
        .reshape(channels_in, depth_len, rows_len, cols_len)
    )
    grad_one = taps_grad(padded_in, hidden_grad, depth_len, rows_len, cols_len)
    grad_two = taps_grad(padded_hidden, upstream, depth_len, rows_len, cols_len)
    grad_bias = jnp.sum(hidden_grad.astype(jnp.float32), 1)
    grad_one, grad_two, grad_bias = total([grad_one, grad_two, grad_bias])
    return (
        grad_features,
        grad_one / voxels_total,
        grad_bias / voxels_total,
        grad_two / voxels_total,
    )


def solution(mesh):
    return jax.shard_map(
        shards,
        mesh=mesh,
        in_specs=(P(None, "gz", "gy", "gx"), P("gz", "gy", "gx"), P(), P(), P()),
        out_specs=(P(None, "gz", "gy", "gx"), P(), P(), P()),
        check_vma=False,
    )
```

```python
import functools

import jax
import jax.numpy as jnp
from jax import lax
from jax.experimental import pallas as pl
from jax.experimental.pallas import tpu as pltpu
from jax.sharding import PartitionSpec as P

EMBED = 16
CHANNELS = 48
LANES = 128
WIDE = 2 * LANES
CELLS = 512
GROUPS = 4
ROW_COLS = 512
VOXELS = 262144.0
SEGMENTS = 2048.0
pull_margin = 4.0
push_margin = 8.0
f32, bf16 = jnp.float32, jnp.bfloat16


def kernel_call(body, outs, scratch=(), scalars=0, flops=0):
    def call(*args):
        specs = [pl.BlockSpec(memory_space=pltpu.SMEM)] * scalars
        specs += [pl.BlockSpec(memory_space=pltpu.VMEM)] * (len(args) - scalars)
        return pl.pallas_call(
            body,
            out_shape=[jax.ShapeDtypeStruct(shape, dtype) for shape, dtype in outs],
            in_specs=specs,
            out_specs=[pl.BlockSpec(memory_space=pltpu.VMEM)] * len(outs),
            scratch_shapes=[pltpu.VMEM(shape, dtype) for shape, dtype in scratch],
            compiler_params=pltpu.CompilerParams(vmem_limit_bytes=40 * 1024 * 1024),
        )(*args)

    return call


def lane(shape):
    return lax.broadcasted_iota(jnp.int32, shape, len(shape) - 1)


def edges(rows):
    at = lane(rows[0].shape)
    first = jnp.zeros(rows[0].shape, f32)
    last = jnp.zeros(rows[0].shape, f32)
    for r, row in enumerate(rows):
        turned = row.astype(f32) if r == 0 else pltpu.roll(row.astype(f32), 8 * r, 1)
        first = jnp.where((at >= 8 * r) & (at < 8 * r + 2), turned, first)
        start = (8 * r - 2) % LANES
        last = jnp.where((at >= start) & (at < start + 2), turned, last)
    return first.astype(bf16), last.astype(bf16)


def widen(blocks, wide_ref):
    for yb, ref in enumerate(blocks):
        for zb in range(3):
            pack = ref[zb, 4].astype(f32)
            for r in range(4):
                edge = pack if r == 0 else pltpu.roll(pack, LANES - 8 * r, 1)
                z, y = 2 * zb + r // 2, 2 * yb + r % 2
                wide_ref[z, y, :, 0:LANES] = ref[zb, r]
                wide_ref[z, y, :, LANES:WIDE] = edge.astype(bf16)


def window(ref, z, y):
    size = ref.shape[2]
    return jnp.concatenate([ref[z + a, y : y + 3].reshape(3 * size, WIDE) for a in range(3)], axis=0)


def fold(taps):
    size = taps.shape[0] // 3
    return pltpu.roll(taps[:size], 1, 1) + taps[size : 2 * size] + pltpu.roll(taps[2 * size :], WIDE - 1, 1)


def split(value):
    high = value.astype(bf16)
    return high, (value - high.astype(f32)).astype(bf16)


def hot(cell):
    return jnp.where(lax.broadcasted_iota(jnp.int32, (CELLS, cell.shape[1]), 0) == cell, 1.0, 0.0).astype(bf16)


def scatter(values, ids):
    group, cell = ids >> 9, ids & (CELLS - 1)
    spread = jnp.concatenate([jnp.where(group == g, values, 0.0) for g in range(GROUPS)], axis=0)
    size = spread.shape[0]
    both = jnp.concatenate(split(spread), axis=0)
    sums = lax.dot_general(both, hot(cell), (((1,), (1,)), ((), ())), preferred_element_type=f32)
    return sums[:size] + sums[size:]


def gather(table, ids):
    group, cell = ids >> 9, ids & (CELLS - 1)
    size = table.shape[0]
    both = jnp.concatenate(split(table), axis=0)
    found = jnp.dot(both, hot(cell), preferred_element_type=f32)
    found = found[:size] + found[size:]
    part = size // GROUPS
    picked = jnp.where(group == 0, found[:part], 0.0)
    for g in range(1, GROUPS):
        picked = picked + jnp.where(group == g, found[g * part : (g + 1) * part], 0.0)
    return picked


def store_tiles(tiles_ref, array):
    rows, cols = array.shape[0] // 8, array.shape[1] // LANES
    for i in range(rows):
        for k in range(cols):
            tiles_ref[i * cols + k] = array[8 * i : 8 * i + 8, LANES * k : LANES * (k + 1)]


def load_tiles(tiles_ref, first, count):
    cols = 4
    return jnp.concatenate(
        [jnp.concatenate([tiles_ref[i * cols + k] for k in range(cols)], axis=1) for i in range(first, first + count)],
        axis=0,
    )


def edge_kernel(rows_ref, first_ref, last_ref):
    first_ref[...], last_ref[...] = edges([rows_ref[r] for r in range(4)])


def embed_kernel(place, low, mid, high, taps_one, taps_two, bias, ids_ref, wide_ref, hidden_ref, embed_ref, tiles_ref):
    widen((low, mid, high), wide_ref)
    gz, gy, gx = place[0], place[1], place[2]
    at = lane((CHANNELS, WIDE))
    inside = (at < LANES) | ((at == LANES) & (gx < place[6])) | ((at == WIDE - 1) & (gx > 0))

    def layer(z, carry):
        for y in range(4):
            folded = fold(jnp.dot(taps_one[...], window(wide_ref, z, y), preferred_element_type=f32))
            folded = jnp.maximum(folded + bias[...], 0.0)
            depth, row = 2 * gz - 1 + z, 2 * gy - 1 + y
            exists = (depth >= 0) & (depth < 2 * place[4] + 2) & (row >= 0) & (row < 2 * place[5] + 2)
            hidden_ref[z, y] = jnp.where(inside & exists, folded, 0.0).astype(bf16)
        return carry

    lax.fori_loop(0, 4, layer, 0)
    for r in range(4):
        folded = fold(jnp.dot(taps_two[...], window(hidden_ref, r // 2, r % 2), preferred_element_type=f32))
        embed_ref[:, LANES * r : LANES * (r + 1)] = folded[:, :LANES]
    row = lax.broadcasted_iota(jnp.int32, (16, CELLS), 0)
    values = jnp.concatenate([embed_ref[...], jnp.where(row == 0, 1.0, 0.0)], axis=0)
    store_tiles(tiles_ref, scatter(values, ids_ref[...]))


def direct_kernel(place, tiles_ref, embed_ref, ids_ref, direct_ref, share_ref, out_ref):
    centers, table = [], []
    for g in range(GROUPS):
        part = load_tiles(tiles_ref, 4 * g, 3)
        counts = part[EMBED : EMBED + 1]
        centers.append(part[:EMBED] / counts)
        row = lax.broadcasted_iota(jnp.int32, (16, CELLS), 0)
        table += [centers[g], jnp.where(row == 0, 1.0 / counts, 0.0)]
    near = gather(jnp.concatenate(table, axis=0), ids_ref[...])
    share = near[EMBED : EMBED + 1]
    offset = embed_ref[...] - near[:EMBED]
    hinge = jnp.maximum(jnp.sum(offset * offset, axis=0, keepdims=True) - pull_margin, 0.0)
    direct = (4.0 / SEGMENTS) * hinge * share * offset
    direct_ref[...] = direct
    share_ref[...] = jnp.broadcast_to(share, share_ref.shape)
    sums = scatter(direct, ids_ref[...])
    mine = lane((EMBED, CELLS)) == place[3]
    scale = 8.0 / (SEGMENTS * (SEGMENTS - 1.0))
    for g in range(GROUPS):
        own = jnp.sum(jnp.where(mine, centers[g], 0.0), axis=1, keepdims=True)
        total = jnp.zeros((EMBED, CELLS), f32)
        for other in centers:
            difference = own - other
            distance = jnp.sum(difference * difference, axis=0, keepdims=True)
            total = total + jnp.maximum(push_margin - distance, 0.0) * difference
        push = -scale * jnp.sum(total, axis=1, keepdims=True)
        grad = jnp.where(mine, push, 0.0) - sums[EMBED * g : EMBED * (g + 1)]
        for i in range(2):
            for k in range(4):
                out_ref[(2 * g + i) * 4 + k] = grad[8 * i : 8 * i + 8, LANES * k : LANES * (k + 1)]


def upstream_kernel(tiles_ref, direct_ref, share_ref, ids_ref, rows_ref, first_ref, last_ref):
    found = gather(load_tiles(tiles_ref, 0, 8), ids_ref[...])
    upstream = (VOXELS * (direct_ref[...] + found * share_ref[0:1])).astype(bf16)
    rows = [upstream[:, LANES * r : LANES * (r + 1)] for r in range(4)]
    for r in range(4):
        rows_ref[r] = rows[r]
    first_ref[...], last_ref[...] = edges(rows)


def backward_kernel(low, mid, high, wide_ref, hidden_ref, taps_two, taps_one, features_ref, tiles_ref, up_ref, grad_ref):
    widen((low, mid, high), up_ref)

    def layer(z, carry):
        for y in range(4):
            folded = fold(jnp.dot(taps_two[...], window(up_ref, z, y), preferred_element_type=f32))
            grad_ref[z, y] = jnp.where(hidden_ref[z, y].astype(f32) > 0.0, folded, 0.0).astype(bf16)
        return carry

    lax.fori_loop(0, 4, layer, 0)
    over_cells = (((1,), (1,)), ((), ()))
    one = jnp.zeros((3 * CHANNELS, 9 * CHANNELS + 16), f32)
    two = jnp.zeros((3 * EMBED, 9 * CHANNELS), f32)

    def shifted(row):
        row = jnp.where(lane(row.shape) < LANES, row.astype(f32), 0.0)
        return jnp.concatenate([pltpu.roll(row, WIDE - 1, 1), row, pltpu.roll(row, 1, 1)], axis=0).astype(bf16)

    for r in range(4):
        z, y = r // 2, r % 2
        folded = fold(jnp.dot(taps_one[...], window(grad_ref, z, y), preferred_element_type=f32))
        features_ref[r] = folded[:, :LANES].astype(bf16)
        seen = jnp.concatenate([window(wide_ref, z + 1, y + 1), jnp.ones((16, WIDE), bf16)], axis=0)
        one = one + lax.dot_general(shifted(grad_ref[z + 1, y + 1]), seen, over_cells, preferred_element_type=f32)
        two = two + lax.dot_general(
            shifted(up_ref[z + 2, y + 2]), window(hidden_ref, z, y), over_cells, preferred_element_type=f32
        )
    one = jnp.concatenate([one, jnp.zeros((3 * CHANNELS, 64), f32)], axis=1)
    two = jnp.concatenate([two, jnp.zeros((3 * EMBED, 80), f32)], axis=1)
    store_tiles(tiles_ref, jnp.concatenate([one, two], axis=0))


def result_kernel(tiles_ref, one_ref, bias_ref, two_ref):
    for c in range(3):
        part = load_tiles(tiles_ref, 6 * c, 6) * (1.0 / VOXELS)
        for ab in range(9):
            one_ref[ab * 3 + c] = part[:, CHANNELS * ab : CHANNELS * (ab + 1)]
        if c == 1:
            bias_ref[...] = part[:, 9 * CHANNELS : 9 * CHANNELS + 1]
        part = load_tiles(tiles_ref, 18 + 2 * c, 2) * (1.0 / VOXELS)
        for ab in range(9):
            two_ref[ab * 3 + c] = part[:, CHANNELS * ab : CHANNELS * (ab + 1)]


def passed(low, high, axis):
    count = lax.axis_size(axis)
    forward = [(i, i + 1) for i in range(count - 1)]
    backward = [(target, source) for source, target in forward]
    return lax.ppermute(high, axis, forward), lax.ppermute(low, axis, backward)


def surround(rows, first, last):
    left, right = passed(first, last, "gx")
    block = jnp.concatenate([rows, (left + right)[None]], axis=0)
    low, high = passed(block, block, "gz")
    block = jnp.stack([low, block, high])
    low, high = passed(block, block, "gy")
    return low, block, high


def total(tiles):
    plane = lax.axis_size(("gy", "gx"))
    depth = lax.axis_size("gz")
    lines = tiles.shape[0] // plane * 8
    pieces = tiles.reshape(plane, lines, LANES)
    piece = jnp.sum(lax.all_to_all(pieces, ("gy", "gx"), 0, 0), 0)
    pieces = jnp.broadcast_to(piece[None], (depth, lines, LANES))
    piece = jnp.sum(lax.all_to_all(pieces, "gz", 0, 0), 0)
    pieces = jnp.broadcast_to(piece[None], (plane, lines, LANES))
    return lax.all_to_all(pieces, ("gy", "gx"), 0, 0).reshape(tiles.shape)


def shards(features, segment_ids, kernel_one, bias_one, kernel_two):
    axes = ("gz", "gy", "gx")
    place = jnp.stack(
        [lax.axis_index(axis) for axis in axes]
        + [lax.axis_index(axes)]
        + [jnp.int32(lax.axis_size(axis) - 1) for axis in axes]
    ).astype(jnp.int32)
    taps_one = jnp.transpose(kernel_one, (2, 3, 0, 1, 4)).reshape(3 * CHANNELS, 9 * CHANNELS)
    taps_two = jnp.transpose(kernel_two, (2, 3, 0, 1, 4)).reshape(3 * EMBED, 9 * CHANNELS)
    back_one = jnp.transpose(kernel_one[::-1, ::-1, ::-1], (2, 4, 0, 1, 3)).reshape(3 * CHANNELS, 9 * CHANNELS)
    back_two = jnp.transpose(kernel_two[::-1, ::-1, ::-1], (2, 4, 0, 1, 3)).reshape(3 * CHANNELS, 9 * EMBED)
    ids = segment_ids.reshape(1, ROW_COLS)
    rows = jnp.transpose(features, (1, 2, 0, 3)).reshape(4, CHANNELS, LANES)

    first, last = kernel_call(edge_kernel, [((CHANNELS, LANES), bf16)] * 2)(rows)
    low, mid, high = surround(rows, first, last)
    wide, hidden, embedding, tiles = kernel_call(
        embed_kernel,
        [
            ((6, 6, CHANNELS, WIDE), bf16),
            ((4, 4, CHANNELS, WIDE), bf16),
            ((EMBED, CELLS), f32),
            ((64, 8, LANES), f32),
        ],
        scalars=1,
    )(place, low, mid, high, taps_one, taps_two, bias_one[:, None], ids)
    tiles = total(tiles)
    direct, share, tiles = kernel_call(
        direct_kernel, [((EMBED, CELLS), f32), ((8, CELLS), f32), ((32, 8, LANES), f32)], scalars=1
    )(place, tiles, embedding, ids)
    tiles = total(tiles)
    rows, first, last = kernel_call(
        upstream_kernel, [((4, EMBED, LANES), bf16), ((EMBED, LANES), bf16), ((EMBED, LANES), bf16)]
    )(tiles, direct, share, ids)
    low, mid, high = surround(rows, first, last)
    rows, tiles = kernel_call(
        backward_kernel,
        [((4, CHANNELS, LANES), bf16), ((96, 8, LANES), f32)],
        scratch=[((6, 6, EMBED, WIDE), bf16), ((4, 4, CHANNELS, WIDE), bf16)],
    )(low, mid, high, wide, hidden, back_two, back_one)
    grad_features = jnp.transpose(rows.reshape(2, 2, CHANNELS, LANES), (2, 0, 1, 3))
    grad_one, grad_bias, grad_two = kernel_call(
        result_kernel, [((27, CHANNELS, CHANNELS), f32), ((CHANNELS, 1), f32), ((27, EMBED, CHANNELS), f32)]
    )(total(tiles))
    return (
        grad_features,
        grad_one.reshape(3, 3, 3, CHANNELS, CHANNELS),
        grad_bias.reshape(CHANNELS),
        grad_two.reshape(3, 3, 3, EMBED, CHANNELS),
    )


def solution(mesh):
    return jax.shard_map(
        shards,
        mesh=mesh,
        in_specs=(P(None, "gz", "gy", "gx"), P("gz", "gy", "gx"), P(), P(), P()),
        out_specs=(P(None, "gz", "gy", "gx"), P(), P(), P()),
        check_vma=False,
    )
```

```python
import functools

import jax
import jax.numpy as jnp
from jax import lax
from jax.experimental import pallas as pl
from jax.experimental.pallas import tpu as pltpu
from jax.sharding import PartitionSpec as P

EMBED = 16
CHANNELS = 48
LANES = 128
WIDE = 2 * LANES
CELLS = 512
GROUPS = 4
ROW_COLS = 512
VOXELS = 262144.0
SEGMENTS = 2048.0
pull_margin = 4.0
push_margin = 8.0
f32, bf16 = jnp.float32, jnp.bfloat16


def kernel_call(body, outs, scratch=(), scalars=0, flops=0):
    def call(*args):
        specs = [pl.BlockSpec(memory_space=pltpu.SMEM)] * scalars
        specs += [pl.BlockSpec(memory_space=pltpu.VMEM)] * (len(args) - scalars)
        return pl.pallas_call(
            body,
            out_shape=[jax.ShapeDtypeStruct(shape, dtype) for shape, dtype in outs],
            in_specs=specs,
            out_specs=[pl.BlockSpec(memory_space=pltpu.VMEM)] * len(outs),
            scratch_shapes=[pltpu.VMEM(shape, dtype) for shape, dtype in scratch],
            compiler_params=pltpu.CompilerParams(vmem_limit_bytes=40 * 1024 * 1024),
        )(*args)

    return call


def lane(shape):
    return lax.broadcasted_iota(jnp.int32, shape, len(shape) - 1)


def edges(rows):
    at = lane(rows[0].shape)
    first = jnp.zeros(rows[0].shape, f32)
    last = jnp.zeros(rows[0].shape, f32)
    for r, row in enumerate(rows):
        turned = row.astype(f32) if r == 0 else pltpu.roll(row.astype(f32), 8 * r, 1)
        first = jnp.where((at >= 8 * r) & (at < 8 * r + 2), turned, first)
        start = (8 * r - 2) % LANES
        last = jnp.where((at >= start) & (at < start + 2), turned, last)
    return first.astype(rows[0].dtype), last.astype(rows[0].dtype)


def widen(blocks, wide_ref):
    for yb, ref in enumerate(blocks):
        for zb in range(3):
            pack = ref[zb, 4].astype(f32)
            for r in range(4):
                edge = pack if r == 0 else pltpu.roll(pack, LANES - 8 * r, 1)
                z, y = 2 * zb + r // 2, 2 * yb + r % 2
                wide_ref[z, y, :, 0:LANES] = ref[zb, r]
                wide_ref[z, y, :, LANES:WIDE] = edge.astype(bf16)


def window(ref, z, y):
    size = ref.shape[2]
    return jnp.concatenate([ref[z + a, y : y + 3].reshape(3 * size, WIDE) for a in range(3)], axis=0)


def fold(taps):
    size = taps.shape[0] // 3
    return pltpu.roll(taps[:size], 1, 1) + taps[size : 2 * size] + pltpu.roll(taps[2 * size :], WIDE - 1, 1)


def split(value):
    high = value.astype(bf16)
    return high, (value - high.astype(f32)).astype(bf16)


def hot(cell):
    return jnp.where(lax.broadcasted_iota(jnp.int32, (CELLS, cell.shape[1]), 0) == cell, 1.0, 0.0).astype(bf16)


def scatter(values, ids):
    group, cell = ids >> 9, ids & (CELLS - 1)
    spread = jnp.concatenate([jnp.where(group == g, values, 0.0) for g in range(GROUPS)], axis=0)
    size = spread.shape[0]
    both = jnp.concatenate(split(spread), axis=0)
    sums = lax.dot_general(both, hot(cell), (((1,), (1,)), ((), ())), preferred_element_type=f32)
    return sums[:size] + sums[size:]


def gather(both, ids):
    group, cell = ids >> 9, ids & (CELLS - 1)
    size = both.shape[0] // 2
    found = jnp.dot(both, hot(cell), preferred_element_type=f32)
    found = found[:size] + found[size:]
    part = size // GROUPS
    picked = jnp.where(group == 0, found[:part], 0.0)
    for g in range(1, GROUPS):
        picked = picked + jnp.where(group == g, found[g * part : (g + 1) * part], 0.0)
    return picked


def store_tiles(tiles_ref, array, first=0):
    lines = tiles_ref.shape[1]
    rows, cols = array.shape[0] // lines, array.shape[1] // LANES
    for i in range(rows):
        for k in range(cols):
            tile = array[lines * i : lines * (i + 1), LANES * k : LANES * (k + 1)]
            tiles_ref[(first + i) * cols + k] = tile.astype(tiles_ref.dtype)


def load_tiles(tiles_ref, first, count):
    cols = 4
    return jnp.concatenate(
        [
            jnp.concatenate([tiles_ref[i * cols + k].astype(f32) for k in range(cols)], axis=1)
            for i in range(first, first + count)
        ],
        axis=0,
    )


def edge_kernel(rows_ref, first_ref, last_ref):
    first_ref[...], last_ref[...] = edges([rows_ref[r] for r in range(4)])


def embed_kernel(place, low, mid, high, taps_one, taps_two, bias, ids_ref, wide_ref, hidden_ref, embed_ref, tiles_ref):
    widen((low, mid, high), wide_ref)
    gz, gy, gx = place[0], place[1], place[2]
    at = lane((CHANNELS, WIDE))
    inside = (at < LANES) | ((at == LANES) & (gx < place[6])) | ((at == WIDE - 1) & (gx > 0))

    def layer(z, carry):
        for y in range(4):
            folded = fold(jnp.dot(taps_one[...], window(wide_ref, z, y), preferred_element_type=f32))
            folded = jnp.maximum(folded + bias[...], 0.0)
            depth, row = 2 * gz - 1 + z, 2 * gy - 1 + y
            exists = (depth >= 0) & (depth < 2 * place[4] + 2) & (row >= 0) & (row < 2 * place[5] + 2)
            hidden_ref[z, y] = jnp.where(inside & exists, folded, 0.0).astype(bf16)
        return carry

    lax.fori_loop(0, 4, layer, 0)
    for r in range(4):
        folded = fold(jnp.dot(taps_two[...], window(hidden_ref, r // 2, r % 2), preferred_element_type=f32))
        embed_ref[:, LANES * r : LANES * (r + 1)] = folded[:, :LANES]
    row = lax.broadcasted_iota(jnp.int32, (16, CELLS), 0)
    values = jnp.concatenate([embed_ref[...], jnp.where(row == 0, 1.0, 0.0)], axis=0)
    store_tiles(tiles_ref, scatter(values, ids_ref[...]))


def direct_kernel(place, tiles_ref, embed_ref, ids_ref, rows_ref, first_ref, last_ref, shares_ref, out_ref):
    centers, table = [], []
    row = lax.broadcasted_iota(jnp.int32, (16, CELLS), 0)
    for g in range(GROUPS):
        part = load_tiles(tiles_ref, 4 * g, 3)
        counts = part[EMBED : EMBED + 1]
        centers.append(part[:EMBED] / counts)
        shares_ref[EMBED * g : EMBED * (g + 1)] = jnp.broadcast_to(1.0 / counts, (EMBED, CELLS))
        table += [centers[g], jnp.where(row == 0, 1.0 / counts, 0.0)]
    near = gather(jnp.concatenate(split(jnp.concatenate(table, axis=0)), axis=0), ids_ref[...])
    share = near[EMBED : EMBED + 1]
    offset = embed_ref[...] - near[:EMBED]
    hinge = jnp.maximum(jnp.sum(offset * offset, axis=0, keepdims=True) - pull_margin, 0.0)
    direct = (4.0 / SEGMENTS) * hinge * share * offset
    row = lax.broadcasted_iota(jnp.int32, (8, CELLS), 0)
    marks = jnp.where(row == 0, ids_ref[...].astype(f32), jnp.where(row == 1, 1.0, 0.0))
    sent = jnp.concatenate([direct, marks], axis=0)
    rows = [sent[:, LANES * r : LANES * (r + 1)] for r in range(4)]
    for r in range(4):
        rows_ref[r] = rows[r]
    first_ref[...], last_ref[...] = edges(rows)
    sums = scatter(direct, ids_ref[...])
    mine = lane((EMBED, CELLS)) == place[3]
    scale = 8.0 / (SEGMENTS * (SEGMENTS - 1.0))
    for g in range(GROUPS):
        own = jnp.sum(jnp.where(mine, centers[g], 0.0), axis=1, keepdims=True)
        total = jnp.zeros((EMBED, CELLS), f32)
        for other in centers:
            difference = own - other
            distance = jnp.sum(difference * difference, axis=0, keepdims=True)
            total = total + jnp.maximum(push_margin - distance, 0.0) * difference
        push = -scale * jnp.sum(total, axis=1, keepdims=True)
        grad = jnp.where(mine, push, 0.0) - sums[EMBED * g : EMBED * (g + 1)]
        store_tiles(out_ref, grad, g)


def backward_kernel(
    low, mid, high, sums_ref, shares_ref, wide_ref, hidden_ref, taps_two, taps_one, features_ref, tiles_ref, up_ref, grad_ref
):
    table = jnp.concatenate(split(load_tiles(sums_ref, 0, 4) * shares_ref[...]), axis=0)

    for yb, ref in enumerate((low, mid, high)):

        def block(zb, carry):
            sent = jnp.concatenate([ref[zb, r] for r in range(5)], axis=1)
            ids = sent[EMBED : EMBED + 1].astype(jnp.int32)
            found = gather(table, ids) * sent[EMBED + 1 : EMBED + 2]
            upstream = VOXELS * (sent[:EMBED] + found)
            pack = upstream[:, 4 * LANES :]
            for r in range(4):
                edge = pack if r == 0 else pltpu.roll(pack, LANES - 8 * r, 1)
                z, y = 2 * zb + r // 2, 2 * yb + r % 2
                up_ref[z, y, :, 0:LANES] = upstream[:, LANES * r : LANES * (r + 1)].astype(bf16)
                up_ref[z, y, :, LANES:WIDE] = edge.astype(bf16)
            return carry

        lax.fori_loop(0, 3, block, 0)

    def layer(z, carry):
        for y in range(4):
            folded = fold(jnp.dot(taps_two[...], window(up_ref, z, y), preferred_element_type=f32))
            grad_ref[z, y] = jnp.where(hidden_ref[z, y].astype(f32) > 0.0, folded, 0.0).astype(bf16)
        return carry

    lax.fori_loop(0, 4, layer, 0)
    over_cells = (((1,), (1,)), ((), ()))
    one = jnp.zeros((3 * CHANNELS, 9 * CHANNELS + 16), f32)
    two = jnp.zeros((3 * EMBED, 9 * CHANNELS), f32)

    def shifted(row):
        row = jnp.where(lane(row.shape) < LANES, row.astype(f32), 0.0)
        return jnp.concatenate([pltpu.roll(row, WIDE - 1, 1), row, pltpu.roll(row, 1, 1)], axis=0).astype(bf16)

    for r in range(4):
        z, y = r // 2, r % 2
        folded = fold(jnp.dot(taps_one[...], window(grad_ref, z, y), preferred_element_type=f32))
        features_ref[r] = folded[:, :LANES].astype(bf16)
        seen = jnp.concatenate([window(wide_ref, z + 1, y + 1), jnp.ones((16, WIDE), bf16)], axis=0)
        one = one + lax.dot_general(shifted(grad_ref[z + 1, y + 1]), seen, over_cells, preferred_element_type=f32)
        two = two + lax.dot_general(
            shifted(up_ref[z + 2, y + 2]), window(hidden_ref, z, y), over_cells, preferred_element_type=f32
        )
    one = jnp.concatenate([one, jnp.zeros((3 * CHANNELS, 64), f32)], axis=1)
    two = jnp.concatenate([two, jnp.zeros((3 * EMBED, 80), f32)], axis=1)
    store_tiles(tiles_ref, jnp.concatenate([one, two, jnp.zeros((64, 512), f32)], axis=0))


def result_kernel(tiles_ref, one_ref, bias_ref, two_ref):
    for c in range(3):
        part = load_tiles(tiles_ref, 3 * c, 3) * (1.0 / VOXELS)
        for ab in range(9):
            one_ref[ab * 3 + c] = part[:, CHANNELS * ab : CHANNELS * (ab + 1)]
        if c == 1:
            bias_ref[...] = part[:, 9 * CHANNELS : 9 * CHANNELS + 1]
        part = load_tiles(tiles_ref, 9 + c, 1) * (1.0 / VOXELS)
        for ab in range(9):
            two_ref[ab * 3 + c] = part[:, CHANNELS * ab : CHANNELS * (ab + 1)]


def passed(low, high, axis):
    count = lax.axis_size(axis)
    forward = [(i, i + 1) for i in range(count - 1)]
    backward = [(target, source) for source, target in forward]
    return lax.ppermute(high, axis, forward), lax.ppermute(low, axis, backward)


def surround(rows, first, last, between=()):
    between = list(between) + [lambda held: held] * 3
    left, right = passed(first, last, "gx")
    left, right = between[0]((left, right))
    block = jnp.concatenate([rows, (left + right)[None]], axis=0)
    low, high = passed(block, block, "gz")
    low, high = between[1]((low, high))
    block = jnp.stack([low, block, high])
    low, high = passed(block, block, "gy")
    low, high = between[2]((low, high))
    return low, block, high


def add_up(pieces):
    return jnp.sum(pieces.astype(f32), 0).astype(pieces.dtype)


def copies(piece, axes):
    return jnp.broadcast_to(piece[None], (lax.axis_size(axes),) + piece.shape)


def steps(tiles, outer, inner):
    held = [tiles.reshape(lax.axis_size(outer), -1, LANES)]

    def scattered(other):
        other, pieces = lax.optimization_barrier((other, lax.all_to_all(held[0], outer, 0, 0)))
        held[0] = copies(add_up(pieces), inner)
        return other

    def exchanged(other):
        other, pieces = lax.optimization_barrier((other, lax.all_to_all(held[0], inner, 0, 0)))
        held[0] = copies(add_up(pieces), outer)
        return other

    def gathered(other):
        other, pieces = lax.optimization_barrier((other, lax.all_to_all(held[0], outer, 0, 0)))
        held[0] = pieces.reshape(tiles.shape)
        return other

    return (scattered, exchanged, gathered), held


def total(tiles, outer, inner):
    moves, held = steps(tiles, outer, inner)
    for move in moves:
        move(())
    return held[0]


def shards(features, segment_ids, kernel_one, bias_one, kernel_two):
    axes = ("gz", "gy", "gx")
    place = jnp.stack(
        [lax.axis_index(axis) for axis in axes]
        + [lax.axis_index(axes)]
        + [jnp.int32(lax.axis_size(axis) - 1) for axis in axes]
    ).astype(jnp.int32)
    taps_one = jnp.transpose(kernel_one, (2, 3, 0, 1, 4)).reshape(3 * CHANNELS, 9 * CHANNELS)
    taps_two = jnp.transpose(kernel_two, (2, 3, 0, 1, 4)).reshape(3 * EMBED, 9 * CHANNELS)
    back_one = jnp.transpose(kernel_one[::-1, ::-1, ::-1], (2, 4, 0, 1, 3)).reshape(3 * CHANNELS, 9 * CHANNELS)
    back_two = jnp.transpose(kernel_two[::-1, ::-1, ::-1], (2, 4, 0, 1, 3)).reshape(3 * CHANNELS, 9 * EMBED)
    ids = segment_ids.reshape(1, ROW_COLS)
    rows = jnp.transpose(features, (1, 2, 0, 3)).reshape(4, CHANNELS, LANES)

    first, last = kernel_call(edge_kernel, [((CHANNELS, LANES), bf16)] * 2)(rows)
    low, mid, high = surround(rows, first, last)
    wide, hidden, embedding, tiles = kernel_call(
        embed_kernel,
        [
            ((6, 6, CHANNELS, WIDE), bf16),
            ((4, 4, CHANNELS, WIDE), bf16),
            ((EMBED, CELLS), f32),
            ((64, 8, LANES), f32),
        ],
        scalars=1,
    )(place, low, mid, high, taps_one, taps_two, bias_one[:, None], ids)
    tiles = total(tiles, ("gy", "gx"), "gz")
    rows, first, last, shares, tiles = kernel_call(
        direct_kernel,
        [
            ((4, 24, LANES), f32),
            ((24, LANES), f32),
            ((24, LANES), f32),
            ((GROUPS * EMBED, CELLS), f32),
            ((16, 16, LANES), bf16),
        ],
        scalars=1,
    )(place, tiles, embedding, ids)
    moves, held = steps(tiles, "gz", ("gy", "gx"))
    low, mid, high = surround(rows, first, last, moves)
    rows, tiles = kernel_call(
        backward_kernel,
        [((4, CHANNELS, LANES), bf16), ((64, 16, LANES), bf16)],
        scratch=[((6, 6, EMBED, WIDE), bf16), ((4, 4, CHANNELS, WIDE), bf16)],
    )(low, mid, high, held[0], shares, wide, hidden, back_two, back_one)
    grad_features = jnp.transpose(rows.reshape(2, 2, CHANNELS, LANES), (2, 0, 1, 3))
    grad_one, grad_bias, grad_two = kernel_call(
        result_kernel, [((27, CHANNELS, CHANNELS), f32), ((CHANNELS, 1), f32), ((27, EMBED, CHANNELS), f32)]
    )(total(tiles, ("gy", "gx"), "gz"))
    return (
        grad_features,
        grad_one.reshape(3, 3, 3, CHANNELS, CHANNELS),
        grad_bias.reshape(CHANNELS),
        grad_two.reshape(3, 3, 3, EMBED, CHANNELS),
    )


def solution(mesh):
    return jax.shard_map(
        shards,
        mesh=mesh,
        in_specs=(P(None, "gz", "gy", "gx"), P("gz", "gy", "gx"), P(), P(), P()),
        out_specs=(P(None, "gz", "gy", "gx"), P(), P(), P()),
        check_vma=False,
    )
```

```python
import functools

import jax
import jax.numpy as jnp
from jax import lax
from jax.experimental import pallas as pl
from jax.experimental.pallas import tpu as pltpu
from jax.sharding import PartitionSpec as P

EMBED = 16
CHANNELS = 48
LANES = 128
WIDE = 2 * LANES
CELLS = 512
GROUPS = 4
ROW_COLS = 512
VOXELS = 262144.0
SEGMENTS = 2048.0
pull_margin = 4.0
push_margin = 8.0
f32, bf16 = jnp.float32, jnp.bfloat16


def kernel_call(body, outs, scratch=(), scalars=0, flops=0):
    def call(*args):
        specs = [pl.BlockSpec(memory_space=pltpu.SMEM)] * scalars
        specs += [pl.BlockSpec(memory_space=pltpu.VMEM)] * (len(args) - scalars)
        return pl.pallas_call(
            body,
            out_shape=[jax.ShapeDtypeStruct(shape, dtype) for shape, dtype in outs],
            in_specs=specs,
            out_specs=[pl.BlockSpec(memory_space=pltpu.VMEM)] * len(outs),
            scratch_shapes=[pltpu.VMEM(shape, dtype) for shape, dtype in scratch],
            compiler_params=pltpu.CompilerParams(vmem_limit_bytes=40 * 1024 * 1024),
        )(*args)

    return call


def lane(shape):
    return lax.broadcasted_iota(jnp.int32, shape, len(shape) - 1)


def edges(rows):
    at = lane(rows[0].shape)
    first = jnp.zeros(rows[0].shape, f32)
    last = jnp.zeros(rows[0].shape, f32)
    for r, row in enumerate(rows):
        turned = row if r == 0 else pltpu.roll(row, 8 * r, 1)
        first = jnp.where((at >= 8 * r) & (at < 8 * r + 4), turned, first)
        start = (8 * r - 4) % LANES
        last = jnp.where((at >= start) & (at < start + 4), turned, last)
    return first, last


def widen(blocks, wide_ref):
    for yb, ref in enumerate(blocks):
        for zb in range(3):
            pack = ref[zb, 4].astype(f32)
            for r in range(4):
                edge = pack if r == 0 else pltpu.roll(pack, LANES - 8 * r, 1)
                z, y = 2 * zb + r // 2, 2 * yb + r % 2
                wide_ref[z, y, :, 0:LANES] = ref[zb, r]
                wide_ref[z, y, :, LANES:WIDE] = edge.astype(bf16)


def window(ref, z, y):
    size = ref.shape[2]
    return jnp.concatenate([ref[z + a, y : y + 3].reshape(3 * size, WIDE) for a in range(3)], axis=0)


def fold(taps):
    size = taps.shape[0] // 3
    return pltpu.roll(taps[:size], 1, 1) + taps[size : 2 * size] + pltpu.roll(taps[2 * size :], WIDE - 1, 1)


def split(value):
    high = value.astype(bf16)
    return high, (value - high.astype(f32)).astype(bf16)


def hot(cell):
    return jnp.where(lax.broadcasted_iota(jnp.int32, (CELLS, cell.shape[1]), 0) == cell, 1.0, 0.0).astype(bf16)


def scatter(values, ids, more=()):
    group, cell = ids >> 9, ids & (CELLS - 1)
    spread = jnp.concatenate([jnp.where(group == g, values, 0.0) for g in range(GROUPS)], axis=0)
    size = spread.shape[0]
    both = jnp.concatenate(split(spread) + tuple(more), axis=0)
    sums = lax.dot_general(both, hot(cell), (((1,), (1,)), ((), ())), preferred_element_type=f32)
    return sums[:size] + sums[size : 2 * size], sums[2 * size :]


def gather(parts, ids):
    group, cell = ids >> 9, ids & (CELLS - 1)
    size = parts[0].shape[0]
    found = jnp.dot(jnp.concatenate(parts, axis=0), hot(cell), preferred_element_type=f32)
    found = sum(found[size * i : size * (i + 1)] for i in range(1, len(parts))) + found[:size]
    part = size // GROUPS
    picked = jnp.where(group == 0, found[:part], 0.0)
    for g in range(1, GROUPS):
        picked = picked + jnp.where(group == g, found[g * part : (g + 1) * part], 0.0)
    return picked


def store_lines(lines_ref, array):
    cols = array.shape[1] // LANES
    for i in range(array.shape[0] // 8):
        for k in range(cols):
            start = 8 * (i * cols + k)
            lines_ref[start : start + 8, 0, :] = array[8 * i : 8 * i + 8, LANES * k : LANES * (k + 1)]


def load_lines(lines_ref, first, count):
    cols = 4
    return jnp.concatenate(
        [
            jnp.concatenate([lines_ref[8 * (i * cols + k) : 8 * (i * cols + k) + 8, 0, :] for k in range(cols)], axis=1)
            for i in range(first, first + count)
        ],
        axis=0,
    )


def store_tiles(tiles_ref, array, first=0):
    lines = tiles_ref.shape[1]
    rows, cols = array.shape[0] // lines, array.shape[1] // LANES
    for i in range(rows):
        for k in range(cols):
            tile = array[lines * i : lines * (i + 1), LANES * k : LANES * (k + 1)]
            tiles_ref[(first + i) * cols + k] = tile.astype(tiles_ref.dtype)


def load_tiles(tiles_ref, first, count):
    cols = 4
    return jnp.concatenate(
        [
            jnp.concatenate([tiles_ref[i * cols + k].astype(f32) for k in range(cols)], axis=1)
            for i in range(first, first + count)
        ],
        axis=0,
    )


def edge_kernel(rows_ref, ids_ref, first_ref, last_ref):
    row = lax.broadcasted_iota(jnp.int32, (16, ROW_COLS), 0)
    ids = ids_ref[...]
    marks = jnp.where(row == 0, ids >> 8, jnp.where(row == 1, ids & 255, jnp.where(row == 2, 1, 0))).astype(f32)
    rows = [
        jnp.concatenate([rows_ref[r].astype(f32), marks[:, LANES * r : LANES * (r + 1)]], axis=0) for r in range(4)
    ]
    first, last = edges(rows)
    first_ref[...] = first.astype(bf16)
    last_ref[...] = last.astype(bf16)


def embed_kernel(place, low, mid, high, taps_one, taps_two, bias, ids_ref, wide_ref, hidden_ref, embed_ref, lines_ref):
    widen((low, mid, high), wide_ref)
    gz, gy, gx = place[0], place[1], place[2]
    at = lane((CHANNELS, WIDE))
    inside = (at < LANES) | ((at < LANES + 3) & (gx < place[6])) | ((at >= WIDE - 3) & (gx > 0))

    def layer(z, carry):
        for y in range(4):
            folded = fold(jnp.dot(taps_one[...], window(wide_ref, z, y), preferred_element_type=f32))
            folded = jnp.maximum(folded + bias[...], 0.0)
            depth, row = 2 * gz - 1 + z, 2 * gy - 1 + y
            exists = (depth >= 0) & (depth < 2 * place[4] + 2) & (row >= 0) & (row < 2 * place[5] + 2)
            hidden_ref[z, y] = jnp.where(inside & exists, folded, 0.0).astype(bf16)
        return carry

    lax.fori_loop(0, 4, layer, 0)
    pack = jnp.zeros((EMBED, LANES), f32)
    at = lane((EMBED, LANES))
    for r in range(4):
        folded = fold(jnp.dot(taps_two[...], window(hidden_ref, r // 2, r % 2), preferred_element_type=f32))
        embed_ref[:, LANES * r : LANES * (r + 1)] = folded[:, :LANES]
        edge = folded[:, LANES:] if r == 0 else pltpu.roll(folded[:, LANES:], 8 * r, 1)
        pack = jnp.where(((at - 8 * r + 4) & (LANES - 1)) < 8, edge, pack)
    embed_ref[:, ROW_COLS:] = pack
    ids = ids_ref[...]
    row = lax.broadcasted_iota(jnp.int32, (16, CELLS), 0)
    ones = jnp.where((ids >> 9) == row, 1.0, 0.0).astype(bf16)
    sums, counts = scatter(embed_ref[:, :ROW_COLS], ids, (ones,))
    store_lines(lines_ref, jnp.concatenate([sums, counts[:8]], axis=0))


def direct_kernel(place, lines_ref, embed_ref, ids_ref, pack_ref, direct_ref, out_ref):
    centers, table = [], []
    row = lax.broadcasted_iota(jnp.int32, (16, CELLS), 0)
    counts = load_lines(lines_ref, 8, 1)
    for g in range(GROUPS):
        count = counts[g : g + 1]
        centers.append(load_lines(lines_ref, 2 * g, 2) / count)
        table += [centers[g], jnp.where(row == 0, 1.0 / count, 0.0)]
    pack = pack_ref[...].astype(f32)
    pack_ids = (256.0 * pack[0:1] + pack[1:2]).astype(jnp.int32)
    ids = jnp.concatenate([ids_ref[...], pack_ids], axis=1)
    mark = jnp.concatenate([jnp.ones((1, ROW_COLS), f32), pack[2:3]], axis=1)
    near = gather(split(jnp.concatenate(table, axis=0)), ids)
    share = near[EMBED : EMBED + 1] * mark
    offset = embed_ref[...] - near[:EMBED]
    hinge = jnp.maximum(jnp.sum(offset * offset, axis=0, keepdims=True) - pull_margin, 0.0)
    direct = (4.0 / SEGMENTS) * hinge * share * offset
    row = lax.broadcasted_iota(jnp.int32, (8, ids.shape[1]), 0)
    marks = jnp.where(row == 0, ids.astype(f32), jnp.where(row == 1, share, 0.0))
    direct_ref[...] = jnp.concatenate([direct, marks], axis=0)
    sums, _ = scatter(direct[:, :ROW_COLS], ids_ref[...])
    mine = lane((EMBED, CELLS)) == place[3]
    scale = 8.0 / (SEGMENTS * (SEGMENTS - 1.0))
    for g in range(GROUPS):
        own = jnp.sum(jnp.where(mine, centers[g], 0.0), axis=1, keepdims=True)
        total = jnp.zeros((EMBED, CELLS), f32)
        for other in centers:
            difference = own - other
            distance = jnp.sum(difference * difference, axis=0, keepdims=True)
            total = total + jnp.maximum(push_margin - distance, 0.0) * difference
        push = -scale * jnp.sum(total, axis=1, keepdims=True)
        grad = jnp.where(mine, push, 0.0) - sums[EMBED * g : EMBED * (g + 1)]
        store_tiles(out_ref, grad, g)


def backward_layers(hidden_ref, up_ref, taps_two, grad_ref):
    def layer(z, carry):
        for y in range(4):
            folded = fold(jnp.dot(taps_two[...], window(up_ref, z, y), preferred_element_type=f32))
            grad_ref[z, y] = jnp.where(hidden_ref[z, y].astype(f32) > 0.0, folded, 0.0).astype(bf16)
        return carry

    lax.fori_loop(0, 4, layer, 0)


def kernels_kernel(direct_ref, sums_ref, wide_ref, hidden_ref, taps_two, block_ref, tiles_ref, up_ref, grad_ref):
    table = jnp.concatenate(
        [jnp.concatenate([sums_ref[4 * i + k] for k in range(4)], axis=1) for i in range(GROUPS)], axis=0
    )
    direct = direct_ref[...]
    ids = direct[EMBED : EMBED + 1].astype(jnp.int32)
    upstream = VOXELS * (direct[:EMBED] + gather((table,), ids) * direct[EMBED + 1 : EMBED + 2])
    upstream = upstream.astype(bf16)
    for r in range(5):
        block_ref[r] = upstream[:, LANES * r : LANES * (r + 1)]
    up_ref[...] = jnp.zeros(up_ref.shape, bf16)
    for r in range(4):
        up_ref[2 + r // 2, 2 + r % 2, :, 0:LANES] = upstream[:, LANES * r : LANES * (r + 1)]
    backward_layers(hidden_ref, up_ref, taps_two, grad_ref)
    over_cells = (((1,), (1,)), ((), ()))

    def shifted(row):
        row = row.astype(f32)
        return jnp.concatenate([pltpu.roll(row, WIDE - 1, 1), row, pltpu.roll(row, 1, 1)], axis=0).astype(bf16)

    def layer(z, carry):
        one, bias = carry
        for y in range(4):
            moved = shifted(grad_ref[z, y])
            one = one + lax.dot_general(moved, window(wide_ref, z, y), over_cells, preferred_element_type=f32)
            own = moved[CHANNELS : 2 * CHANNELS]
            bias = bias + lax.dot_general(jnp.ones((16, WIDE), bf16), own, over_cells, preferred_element_type=f32)
        return one, bias

    zeros = jnp.zeros((3 * CHANNELS, 9 * CHANNELS), f32), jnp.zeros((16, CHANNELS), f32)
    one, bias = lax.fori_loop(0, 4, layer, zeros)
    two = jnp.zeros((3 * EMBED, 9 * CHANNELS), f32)
    for r in range(4):
        z, y = r // 2, r % 2
        two = two + lax.dot_general(
            shifted(up_ref[z + 2, y + 2]), window(hidden_ref, z, y), over_cells, preferred_element_type=f32
        )
    one = jnp.concatenate([one, jnp.zeros((3 * CHANNELS, 80), f32)], axis=1)
    bias = jnp.concatenate([bias] * 3, axis=0)
    two = jnp.concatenate([two, bias, jnp.zeros((3 * EMBED, 32), f32)], axis=1)
    store_tiles(tiles_ref, jnp.concatenate([one, two], axis=0))


def features_kernel(low, mid, high, hidden_ref, taps_two, taps_one, features_ref, up_ref, grad_ref):
    widen((low, mid, high), up_ref)
    backward_layers(hidden_ref, up_ref, taps_two, grad_ref)
    for r in range(4):
        folded = fold(jnp.dot(taps_one[...], window(grad_ref, r // 2, r % 2), preferred_element_type=f32))
        features_ref[r] = folded[:, :LANES].astype(bf16)


def result_kernel(tiles_ref, one_ref, bias_ref, two_ref):
    whole = load_tiles(tiles_ref, 0, 8) * (1.0 / VOXELS)
    for c in range(3):
        part = whole[CHANNELS * c : CHANNELS * (c + 1)]
        for ab in range(9):
            one_ref[ab * 3 + c] = part[:, CHANNELS * ab : CHANNELS * (ab + 1)]
        part = whole[3 * CHANNELS + EMBED * c : 3 * CHANNELS + EMBED * (c + 1)]
        for ab in range(9):
            two_ref[ab * 3 + c] = part[:, CHANNELS * ab : CHANNELS * (ab + 1)]
    bias_ref[...] = whole[3 * CHANNELS : 3 * CHANNELS + 1, 9 * CHANNELS : 10 * CHANNELS]


def passed(low, high, axis):
    count = lax.axis_size(axis)
    forward = [(i, i + 1) for i in range(count - 1)]
    backward = [(target, source) for source, target in forward]
    return lax.ppermute(high, axis, forward), lax.ppermute(low, axis, backward)


def surround(block, between=None):
    between = between or [lambda held: held] * 2
    low, high = between[0](passed(block, block, "gz"))
    block = jnp.stack([low, block, high])
    low, high = between[1](passed(block, block, "gy"))
    return low, block, high


def add_up(pieces):
    return jnp.sum(pieces.astype(f32), 0).astype(pieces.dtype)


def copies(piece, axes):
    return jnp.broadcast_to(piece[None], (lax.axis_size(axes),) + piece.shape)


def steps(tiles, outer, inner):
    groups = lax.axis_size(outer)
    held = [tiles.reshape((groups, tiles.shape[0] // groups) + tiles.shape[1:])]

    def scattered(other):
        other, pieces = lax.optimization_barrier((other, lax.all_to_all(held[0], outer, 0, 0)))
        held[0] = copies(add_up(pieces), inner)
        return other

    def exchanged(other):
        other, pieces = lax.optimization_barrier((other, lax.all_to_all(held[0], inner, 0, 0)))
        held[0] = copies(add_up(pieces), outer)
        return other

    def gathered(other):
        other, pieces = lax.optimization_barrier((other, lax.all_to_all(held[0], outer, 0, 0)))
        held[0] = pieces.reshape(tiles.shape)
        return other

    return (scattered, exchanged, gathered), held


def total(tiles, outer, inner):
    moves, held = steps(tiles, outer, inner)
    for move in moves:
        move(())
    return held[0]


def shards(features, segment_ids, kernel_one, bias_one, kernel_two):
    axes = ("gz", "gy", "gx")
    place = jnp.stack(
        [lax.axis_index(axis) for axis in axes]
        + [lax.axis_index(axes)]
        + [jnp.int32(lax.axis_size(axis) - 1) for axis in axes]
    ).astype(jnp.int32)
    taps_one = jnp.transpose(kernel_one, (2, 3, 0, 1, 4)).reshape(3 * CHANNELS, 9 * CHANNELS)
    taps_two = jnp.transpose(kernel_two, (2, 3, 0, 1, 4)).reshape(3 * EMBED, 9 * CHANNELS)
    back_one = jnp.transpose(kernel_one[::-1, ::-1, ::-1], (2, 4, 0, 1, 3)).reshape(3 * CHANNELS, 9 * CHANNELS)
    back_two = jnp.transpose(kernel_two[::-1, ::-1, ::-1], (2, 4, 0, 1, 3)).reshape(3 * CHANNELS, 9 * EMBED)
    ids = segment_ids.reshape(1, ROW_COLS)
    rows = jnp.transpose(features, (1, 2, 0, 3)).reshape(4, CHANNELS, LANES)

    first, last = kernel_call(edge_kernel, [((CHANNELS + 16, LANES), bf16)] * 2)(rows, ids)
    left, right = passed(first, last, "gx")
    pack = left + right
    low, mid, high = surround(jnp.concatenate([rows, pack[None, :CHANNELS]], axis=0))
    wide, hidden, embedding, lines = kernel_call(
        embed_kernel,
        [
            ((6, 6, CHANNELS, WIDE), bf16),
            ((4, 4, CHANNELS, WIDE), bf16),
            ((EMBED, ROW_COLS + LANES), f32),
            ((288, 1, LANES), f32),
        ],
        scalars=1,
    )(place, low, mid, high, taps_one, taps_two, bias_one[:, None], ids)
    lines = total(lines, ("gy", "gx"), "gz")
    direct, tiles = kernel_call(direct_kernel, [((24, ROW_COLS + LANES), f32), ((16, 16, LANES), bf16)], scalars=1)(
        place, lines, embedding, ids, pack[CHANNELS:]
    )
    tiles = total(tiles, "gz", ("gy", "gx"))
    back = [((6, 6, EMBED, WIDE), bf16), ((4, 4, CHANNELS, WIDE), bf16)]
    block, tiles = kernel_call(
        kernels_kernel, [((5, EMBED, LANES), bf16), ((32, 24, LANES), bf16)], scratch=back
    )(direct, tiles, wide, hidden, back_two)
    moves, held = steps(tiles, ("gy", "gx"), "gz")
    low, mid, high = surround(block, moves)
    (rows,) = kernel_call(features_kernel, [((4, CHANNELS, LANES), bf16)], scratch=back)(
        low, mid, high, hidden, back_two, back_one
    )
    moves[2](())
    grad_features = jnp.transpose(rows.reshape(2, 2, CHANNELS, LANES), (2, 0, 1, 3))
    grad_one, grad_bias, grad_two = kernel_call(
        result_kernel, [((27, CHANNELS, CHANNELS), f32), ((1, CHANNELS), f32), ((27, EMBED, CHANNELS), f32)]
    )(held[0])
    return (
        grad_features,
        grad_one.reshape(3, 3, 3, CHANNELS, CHANNELS),
        grad_bias.reshape(CHANNELS),
        grad_two.reshape(3, 3, 3, EMBED, CHANNELS),
    )


def solution(mesh):
    return jax.shard_map(
        shards,
        mesh=mesh,
        in_specs=(P(None, "gz", "gy", "gx"), P("gz", "gy", "gx"), P(), P(), P()),
        out_specs=(P(None, "gz", "gy", "gx"), P(), P(), P()),
        check_vma=False,
    )
```

```python
import functools

import jax
import jax.numpy as jnp
from jax import lax
from jax.experimental import pallas as pl
from jax.experimental.pallas import tpu as pltpu
from jax.sharding import PartitionSpec as P

EMBED = 16
CHANNELS = 48
LANES = 128
WIDE = 2 * LANES
CELLS = 512
GROUPS = 4
ROW_COLS = 512
VOXELS = 262144.0
SEGMENTS = 2048.0
pull_margin = 4.0
push_margin = 8.0
f32, bf16 = jnp.float32, jnp.bfloat16


def kernel_call(body, outs, scratch=(), scalars=0, flops=0):
    def call(*args):
        specs = [pl.BlockSpec(memory_space=pltpu.SMEM)] * scalars
        specs += [pl.BlockSpec(memory_space=pltpu.VMEM)] * (len(args) - scalars)
        return pl.pallas_call(
            body,
            out_shape=[jax.ShapeDtypeStruct(shape, dtype) for shape, dtype in outs],
            in_specs=specs,
            out_specs=[pl.BlockSpec(memory_space=pltpu.VMEM)] * len(outs),
            scratch_shapes=[pltpu.VMEM(shape, dtype) for shape, dtype in scratch],
            compiler_params=pltpu.CompilerParams(vmem_limit_bytes=40 * 1024 * 1024),
        )(*args)

    return call


def lane(shape):
    return lax.broadcasted_iota(jnp.int32, shape, len(shape) - 1)


def edges(rows):
    at = lane(rows[0].shape)
    first = jnp.zeros(rows[0].shape, f32)
    last = jnp.zeros(rows[0].shape, f32)
    for r, row in enumerate(rows):
        turned = row if r == 0 else pltpu.roll(row, 8 * r, 1)
        first = jnp.where((at >= 8 * r) & (at < 8 * r + 4), turned, first)
        start = (8 * r - 4) % LANES
        last = jnp.where((at >= start) & (at < start + 4), turned, last)
    return first, last


def widen(blocks, wide_ref):
    for yb, ref in enumerate(blocks):
        for zb in range(3):
            pack = ref[zb, 4].astype(f32)
            for r in range(4):
                edge = pack if r == 0 else pltpu.roll(pack, LANES - 8 * r, 1)
                z, y = 2 * zb + r // 2, 2 * yb + r % 2
                wide_ref[z, y, :, 0:LANES] = ref[zb, r]
                wide_ref[z, y, :, LANES:WIDE] = edge.astype(bf16)


def window(ref, z, y):
    size = ref.shape[2]
    return jnp.concatenate([ref[z + a, y : y + 3].reshape(3 * size, WIDE) for a in range(3)], axis=0)


def fold(taps):
    size = taps.shape[0] // 3
    return pltpu.roll(taps[:size], 1, 1) + taps[size : 2 * size] + pltpu.roll(taps[2 * size :], WIDE - 1, 1)


def split(value):
    high = value.astype(bf16)
    return high, (value - high.astype(f32)).astype(bf16)


def hot(cell):
    return jnp.where(lax.broadcasted_iota(jnp.int32, (CELLS, cell.shape[1]), 0) == cell, 1.0, 0.0).astype(bf16)


def scatter(values, ids, more=()):
    group, cell = ids >> 9, ids & (CELLS - 1)
    spread = jnp.concatenate([jnp.where(group == g, values, 0.0) for g in range(GROUPS)], axis=0)
    size = spread.shape[0]
    both = jnp.concatenate(split(spread) + tuple(more), axis=0)
    sums = lax.dot_general(both, hot(cell), (((1,), (1,)), ((), ())), preferred_element_type=f32)
    return sums[:size] + sums[size : 2 * size], sums[2 * size :]


def gather(parts, ids):
    group, cell = ids >> 9, ids & (CELLS - 1)
    size = parts[0].shape[0]
    found = jnp.dot(jnp.concatenate(parts, axis=0), hot(cell), preferred_element_type=f32)
    found = sum(found[size * i : size * (i + 1)] for i in range(1, len(parts))) + found[:size]
    part = size // GROUPS
    picked = jnp.where(group == 0, found[:part], 0.0)
    for g in range(1, GROUPS):
        picked = picked + jnp.where(group == g, found[g * part : (g + 1) * part], 0.0)
    return picked


def store_lines(lines_ref, array):
    cols = array.shape[1] // LANES
    for i in range(array.shape[0] // 8):
        for k in range(cols):
            start = 8 * (i * cols + k)
            lines_ref[start : start + 8, 0, :] = array[8 * i : 8 * i + 8, LANES * k : LANES * (k + 1)]


def load_lines(lines_ref, first, count):
    cols = 4
    return jnp.concatenate(
        [
            jnp.concatenate([lines_ref[8 * (i * cols + k) : 8 * (i * cols + k) + 8, 0, :] for k in range(cols)], axis=1)
            for i in range(first, first + count)
        ],
        axis=0,
    )


def store_tiles(tiles_ref, array, first=0):
    lines = tiles_ref.shape[1]
    rows, cols = array.shape[0] // lines, array.shape[1] // LANES
    for i in range(rows):
        for k in range(cols):
            tile = array[lines * i : lines * (i + 1), LANES * k : LANES * (k + 1)]
            tiles_ref[(first + i) * cols + k] = tile.astype(tiles_ref.dtype)


def load_tiles(tiles_ref, first, count):
    cols = 4
    return jnp.concatenate(
        [
            jnp.concatenate([tiles_ref[i * cols + k].astype(f32) for k in range(cols)], axis=1)
            for i in range(first, first + count)
        ],
        axis=0,
    )


def edge_kernel(features_hbm, ids_hbm, rows_ref, first_ref, last_ref, features_ref, ids_ref, done):
    fetches = [
        pltpu.make_async_copy(features_hbm, features_ref, done.at[0]),
        pltpu.make_async_copy(ids_hbm, ids_ref, done.at[1]),
    ]
    for fetch in fetches:
        fetch.start()
    for fetch in fetches:
        fetch.wait()
    features = features_ref[...].astype(f32)
    row = lax.broadcasted_iota(jnp.int32, (16, LANES), 0)
    rows = []
    for r in range(4):
        mine = features[:, r // 2, r % 2, :]
        rows_ref[r] = mine.astype(bf16)
        ids = ids_ref[r // 2, r % 2 : r % 2 + 1]
        marks = jnp.where(row == 0, ids >> 8, jnp.where(row == 1, ids & 255, jnp.where(row == 2, 1, 0)))
        rows.append(jnp.concatenate([mine, marks.astype(f32)], axis=0))
    first, last = edges(rows)
    first_ref[...] = first.astype(bf16)
    last_ref[...] = last.astype(bf16)


def embed_kernel(place, low, mid, high, taps_one, taps_two, bias, ids_ref, back_one, back_two, marks, *outs):
    wide_ref, hidden_ref, embed_ref, lines_ref = outs
    widen((low, mid, high), wide_ref)
    gz, gy, gx = place[0], place[1], place[2]
    at = lane((CHANNELS, WIDE))
    inside = (at < LANES) | ((at < LANES + 3) & (gx < place[6])) | ((at >= WIDE - 3) & (gx > 0))

    def layer(z, carry):
        for y in range(4):
            folded = fold(jnp.dot(taps_one[...], window(wide_ref, z, y), preferred_element_type=f32))
            folded = jnp.maximum(folded + bias[...], 0.0)
            depth, row = 2 * gz - 1 + z, 2 * gy - 1 + y
            exists = (depth >= 0) & (depth < 2 * place[4] + 2) & (row >= 0) & (row < 2 * place[5] + 2)
            hidden_ref[z, y] = jnp.where(inside & exists, folded, 0.0).astype(bf16)
        return carry

    lax.fori_loop(0, 4, layer, 0)
    pack = jnp.zeros((EMBED, LANES), f32)
    at = lane((EMBED, LANES))
    for r in range(4):
        folded = fold(jnp.dot(taps_two[...], window(hidden_ref, r // 2, r % 2), preferred_element_type=f32))
        embed_ref[:, LANES * r : LANES * (r + 1)] = folded[:, :LANES]
        edge = folded[:, LANES:] if r == 0 else pltpu.roll(folded[:, LANES:], 8 * r, 1)
        pack = jnp.where(((at - 8 * r + 4) & (LANES - 1)) < 8, edge, pack)
    embed_ref[:, ROW_COLS:] = pack
    ids = ids_ref[...]
    row = lax.broadcasted_iota(jnp.int32, (16, CELLS), 0)
    ones = jnp.where((ids >> 9) == row, 1.0, 0.0).astype(bf16)
    sums, counts = scatter(embed_ref[:, :ROW_COLS], ids, (ones,))
    store_lines(lines_ref, jnp.concatenate([sums, counts[:8]], axis=0))


def direct_kernel(place, lines_ref, embed_ref, ids_ref, pack_ref, direct_ref, out_ref):
    centers, table = [], []
    row = lax.broadcasted_iota(jnp.int32, (16, CELLS), 0)
    counts = load_lines(lines_ref, 8, 1)
    for g in range(GROUPS):
        count = counts[g : g + 1]
        centers.append(load_lines(lines_ref, 2 * g, 2) / count)
        table += [centers[g], jnp.where(row == 0, 1.0 / count, 0.0)]
    pack = pack_ref[...].astype(f32)
    pack_ids = (256.0 * pack[0:1] + pack[1:2]).astype(jnp.int32)
    ids = jnp.concatenate([ids_ref[...], pack_ids], axis=1)
    mark = jnp.concatenate([jnp.ones((1, ROW_COLS), f32), pack[2:3]], axis=1)
    near = gather(split(jnp.concatenate(table, axis=0)), ids)
    share = near[EMBED : EMBED + 1] * mark
    offset = embed_ref[...] - near[:EMBED]
    hinge = jnp.maximum(jnp.sum(offset * offset, axis=0, keepdims=True) - pull_margin, 0.0)
    direct = (4.0 / SEGMENTS) * hinge * share * offset
    row = lax.broadcasted_iota(jnp.int32, (8, ids.shape[1]), 0)
    marks = jnp.where(row == 0, ids.astype(f32), jnp.where(row == 1, share, 0.0))
    direct_ref[...] = jnp.concatenate([direct, marks], axis=0)
    sums, _ = scatter(direct[:, :ROW_COLS], ids_ref[...])
    mine = lane((EMBED, CELLS)) == place[3]
    scale = 8.0 / (SEGMENTS * (SEGMENTS - 1.0))
    for g in range(GROUPS):
        own = jnp.sum(jnp.where(mine, centers[g], 0.0), axis=1, keepdims=True)
        total = jnp.zeros((EMBED, CELLS), f32)
        for other in centers:
            difference = own - other
            distance = jnp.sum(difference * difference, axis=0, keepdims=True)
            total = total + jnp.maximum(push_margin - distance, 0.0) * difference
        push = -scale * jnp.sum(total, axis=1, keepdims=True)
        grad = jnp.where(mine, push, 0.0) - sums[EMBED * g : EMBED * (g + 1)]
        store_tiles(out_ref, grad, g)


def backward_layers(hidden_ref, up_ref, taps_two, grad_ref):
    def layer(z, carry):
        for y in range(4):
            folded = fold(jnp.dot(taps_two[...], window(up_ref, z, y), preferred_element_type=f32))
            grad_ref[z, y] = jnp.where(hidden_ref[z, y].astype(f32) > 0.0, folded, 0.0).astype(bf16)
        return carry

    lax.fori_loop(0, 4, layer, 0)


def kernels_kernel(direct_ref, sums_ref, wide_ref, hidden_ref, taps_two, block_ref, tiles_ref, up_ref, grad_ref):
    table = jnp.concatenate(
        [jnp.concatenate([sums_ref[4 * i + k] for k in range(4)], axis=1) for i in range(GROUPS)], axis=0
    )
    direct = direct_ref[...]
    ids = direct[EMBED : EMBED + 1].astype(jnp.int32)
    upstream = VOXELS * (direct[:EMBED] + gather((table,), ids) * direct[EMBED + 1 : EMBED + 2])
    upstream = upstream.astype(bf16)
    for r in range(5):
        block_ref[r] = upstream[:, LANES * r : LANES * (r + 1)]
    up_ref[...] = jnp.zeros(up_ref.shape, bf16)
    for r in range(4):
        up_ref[2 + r // 2, 2 + r % 2, :, 0:LANES] = upstream[:, LANES * r : LANES * (r + 1)]
    backward_layers(hidden_ref, up_ref, taps_two, grad_ref)
    over_cells = (((1,), (1,)), ((), ()))

    def shifted(row):
        row = row.astype(f32)
        return jnp.concatenate([pltpu.roll(row, WIDE - 1, 1), row, pltpu.roll(row, 1, 1)], axis=0).astype(bf16)

    def layer(z, carry):
        one, bias = carry
        moved = jnp.concatenate([shifted(grad_ref[z, y]) for y in range(4)], axis=1)
        seen = jnp.concatenate([window(wide_ref, z, y) for y in range(4)], axis=1)
        one = one + lax.dot_general(moved, seen, over_cells, preferred_element_type=f32)
        for y in range(4):
            bias = bias + grad_ref[z, y].astype(f32)
        return one, bias

    zeros = jnp.zeros((3 * CHANNELS, 9 * CHANNELS), f32), jnp.zeros((CHANNELS, WIDE), f32)
    one, bias = lax.fori_loop(0, 4, layer, zeros)
    ones = jnp.ones((16, 2 * WIDE), bf16)
    bias = jnp.concatenate(split(bias), axis=1)
    bias = lax.dot_general(ones, bias, over_cells, preferred_element_type=f32)
    moved = jnp.concatenate([shifted(up_ref[2 + r // 2, 2 + r % 2]) for r in range(4)], axis=1)
    seen = jnp.concatenate([window(hidden_ref, r // 2, r % 2) for r in range(4)], axis=1)
    two = lax.dot_general(seen, moved, over_cells, preferred_element_type=f32).T
    one = jnp.concatenate([one, jnp.zeros((3 * CHANNELS, 80), f32)], axis=1)
    bias = jnp.concatenate([bias] * 3, axis=0)
    two = jnp.concatenate([two, bias, jnp.zeros((3 * EMBED, 32), f32)], axis=1)
    store_tiles(tiles_ref, jnp.concatenate([one, two], axis=0))


def features_kernel(low, mid, high, hidden_ref, taps_two, taps_one, features_ref, up_ref, grad_ref):
    widen((low, mid, high), up_ref)
    backward_layers(hidden_ref, up_ref, taps_two, grad_ref)
    for r in range(4):
        folded = fold(jnp.dot(taps_one[...], window(grad_ref, r // 2, r % 2), preferred_element_type=f32))
        features_ref[:, r // 2, r % 2, :] = folded[:, :LANES].astype(bf16)


def result_kernel(tiles_ref, one_ref, bias_ref, two_ref):
    whole = load_tiles(tiles_ref, 0, 8) * (1.0 / VOXELS)
    for c in range(3):
        part = whole[CHANNELS * c : CHANNELS * (c + 1)]
        for ab in range(9):
            one_ref[ab * 3 + c] = part[:, CHANNELS * ab : CHANNELS * (ab + 1)]
        part = whole[3 * CHANNELS + EMBED * c : 3 * CHANNELS + EMBED * (c + 1)]
        for ab in range(9):
            two_ref[ab * 3 + c] = part[:, CHANNELS * ab : CHANNELS * (ab + 1)]
    bias_ref[...] = whole[3 * CHANNELS : 3 * CHANNELS + 1, 9 * CHANNELS : 10 * CHANNELS]


def passed(low, high, axis):
    count = lax.axis_size(axis)
    forward = [(i, i + 1) for i in range(count - 1)]
    backward = [(target, source) for source, target in forward]
    return lax.ppermute(high, axis, forward), lax.ppermute(low, axis, backward)


def surround(block, beside=lambda held: held, then=lambda held: held):
    low, high = beside(passed(block, block, "gz"))
    block = jnp.stack([low, block, high])
    low, high = then(passed(block, block, "gy"))
    return low, block, high


def add_up(pieces):
    return jnp.sum(pieces.astype(f32), 0).astype(pieces.dtype)


def copies(piece, axes):
    return jnp.broadcast_to(piece[None], (lax.axis_size(axes),) + piece.shape)


def steps(tiles, outer, inner):
    groups = lax.axis_size(outer)
    held = [tiles.reshape((groups, tiles.shape[0] // groups) + tiles.shape[1:])]

    def scattered(other):
        other, pieces = lax.optimization_barrier((other, lax.all_to_all(held[0], outer, 0, 0)))
        held[0] = copies(add_up(pieces), inner)
        return other

    def exchanged(other):
        other, pieces = lax.optimization_barrier((other, lax.all_to_all(held[0], inner, 0, 0)))
        held[0] = copies(add_up(pieces), outer)
        return other

    def gathered(other):
        other, pieces = lax.optimization_barrier((other, lax.all_to_all(held[0], outer, 0, 0)))
        held[0] = pieces.reshape(tiles.shape)
        return other

    return (scattered, exchanged, gathered), held


def total(tiles, outer, inner):
    moves, held = steps(tiles, outer, inner)
    for move in moves:
        move(())
    return held[0]


def shards(features, segment_ids, kernel_one, bias_one, kernel_two):
    axes = ("gz", "gy", "gx")
    place = jnp.stack(
        [lax.axis_index(axis) for axis in axes]
        + [lax.axis_index(axes)]
        + [jnp.int32(lax.axis_size(axis) - 1) for axis in axes]
    ).astype(jnp.int32)
    taps_one = jnp.transpose(kernel_one, (2, 3, 0, 1, 4)).reshape(3 * CHANNELS, 9 * CHANNELS)
    taps_two = jnp.transpose(kernel_two, (2, 3, 0, 1, 4)).reshape(3 * EMBED, 9 * CHANNELS)
    back_one = jnp.transpose(kernel_one[::-1, ::-1, ::-1], (2, 4, 0, 1, 3)).reshape(3 * CHANNELS, 9 * CHANNELS)
    back_two = jnp.transpose(kernel_two[::-1, ::-1, ::-1], (2, 4, 0, 1, 3)).reshape(3 * CHANNELS, 9 * EMBED)
    ids = segment_ids.reshape(1, ROW_COLS)

    rows, first, last = pl.pallas_call(
        edge_kernel,
        out_shape=[jax.ShapeDtypeStruct((4, CHANNELS, LANES), bf16)]
        + [jax.ShapeDtypeStruct((CHANNELS + 16, LANES), bf16)] * 2,
        in_specs=[pl.BlockSpec(memory_space=pl.ANY)] * 2,
        out_specs=[pl.BlockSpec(memory_space=pltpu.VMEM)] * 3,
        scratch_shapes=[
            pltpu.VMEM(features.shape, bf16),
            pltpu.VMEM(segment_ids.shape, jnp.int32),
            pltpu.SemaphoreType.DMA((2,)),
        ],
    )(features, segment_ids)
    left, right = passed(first, last, "gx")
    pack = left + right
    low, mid, high = surround(jnp.concatenate([rows, pack[None, :CHANNELS]], axis=0))
    marks = pack[CHANNELS:]
    wide, hidden, embedding, lines = kernel_call(
        embed_kernel,
        [
            ((6, 6, CHANNELS, WIDE), bf16),
            ((4, 4, CHANNELS, WIDE), bf16),
            ((EMBED, ROW_COLS + LANES), f32),
            ((288, 1, LANES), f32),
        ],
        scalars=1,
    )(place, low, mid, high, taps_one, taps_two, bias_one[:, None], ids, back_one, back_two, marks)
    lines = total(lines, ("gy", "gx"), "gz")
    direct, tiles = kernel_call(direct_kernel, [((24, ROW_COLS + LANES), f32), ((16, 16, LANES), bf16)], scalars=1)(
        place, lines, embedding, ids, marks
    )
    tiles = total(tiles, "gz", ("gy", "gx"))
    back = [((6, 6, EMBED, WIDE), bf16), ((4, 4, CHANNELS, WIDE), bf16)]
    block, tiles = kernel_call(
        kernels_kernel, [((5, EMBED, LANES), bf16), ((32, 24, LANES), bf16)], scratch=back
    )(direct, tiles, wide, hidden, back_two)
    moves, held = steps(tiles, ("gy", "gx"), "gz")
    low, mid, high = surround(block, *moves[:2])
    (grad_features,) = kernel_call(features_kernel, [((CHANNELS, 2, 2, LANES), bf16)], scratch=back)(
        low, mid, high, hidden, back_two, back_one
    )
    moves[2](())
    grad_one, grad_bias, grad_two = kernel_call(
        result_kernel, [((27, CHANNELS, CHANNELS), f32), ((1, CHANNELS), f32), ((27, EMBED, CHANNELS), f32)]
    )(held[0])
    return (
        grad_features,
        grad_one.reshape(3, 3, 3, CHANNELS, CHANNELS),
        grad_bias.reshape(CHANNELS),
        grad_two.reshape(3, 3, 3, EMBED, CHANNELS),
    )


def solution(mesh):
    return jax.shard_map(
        shards,
        mesh=mesh,
        in_specs=(P(None, "gz", "gy", "gx"), P("gz", "gy", "gx"), P(), P(), P()),
        out_specs=(P(None, "gz", "gy", "gx"), P(), P(), P()),
        check_vma=False,
    )
```

```python
import functools

import jax
import jax.numpy as jnp
from jax import lax
from jax.experimental import pallas as pl
from jax.experimental.pallas import tpu as pltpu
from jax.sharding import PartitionSpec as P

EMBED = 16
CHANNELS = 48
LANES = 128
WIDE = 2 * LANES
CELLS = 512
GROUPS = 4
ROW_COLS = 512
VOXELS = 262144.0
SEGMENTS = 2048.0
pull_margin = 4.0
push_margin = 8.0
f32, bf16 = jnp.float32, jnp.bfloat16


def kernel_call(body, outs, scratch=(), scalars=0, flops=0):
    def call(*args):
        specs = [pl.BlockSpec(memory_space=pltpu.SMEM)] * scalars
        specs += [pl.BlockSpec(memory_space=pltpu.VMEM)] * (len(args) - scalars)
        return pl.pallas_call(
            body,
            out_shape=[jax.ShapeDtypeStruct(shape, dtype) for shape, dtype in outs],
            in_specs=specs,
            out_specs=[pl.BlockSpec(memory_space=pltpu.VMEM)] * len(outs),
            scratch_shapes=[pltpu.VMEM(shape, dtype) for shape, dtype in scratch],
            compiler_params=pltpu.CompilerParams(vmem_limit_bytes=40 * 1024 * 1024),
        )(*args)

    return call


def lane(shape):
    return lax.broadcasted_iota(jnp.int32, shape, len(shape) - 1)


def edges(rows):
    at = lane(rows[0].shape)
    first = jnp.zeros(rows[0].shape, f32)
    last = jnp.zeros(rows[0].shape, f32)
    for r, row in enumerate(rows):
        turned = row if r == 0 else pltpu.roll(row, 8 * r, 1)
        first = jnp.where((at >= 8 * r) & (at < 8 * r + 4), turned, first)
        start = (8 * r - 4) % LANES
        last = jnp.where((at >= start) & (at < start + 4), turned, last)
    return first, last


def widen(blocks, wide_ref):
    for yb, ref in enumerate(blocks):
        for zb in range(3):
            pack = ref[zb, 4].astype(f32)
            for r in range(4):
                edge = pack if r == 0 else pltpu.roll(pack, LANES - 8 * r, 1)
                z, y = 2 * zb + r // 2, 2 * yb + r % 2
                wide_ref[z, y, :, 0:LANES] = ref[zb, r]
                wide_ref[z, y, :, LANES:WIDE] = edge.astype(bf16)


def window(ref, z, y):
    size = ref.shape[2]
    return jnp.concatenate([ref[z + a, y : y + 3].reshape(3 * size, WIDE) for a in range(3)], axis=0)


def fold(taps):
    size = taps.shape[0] // 3
    return pltpu.roll(taps[:size], 1, 1) + taps[size : 2 * size] + pltpu.roll(taps[2 * size :], WIDE - 1, 1)


def split(value):
    high = value.astype(bf16)
    return high, (value - high.astype(f32)).astype(bf16)


def hot(cell):
    return jnp.where(lax.broadcasted_iota(jnp.int32, (CELLS, cell.shape[1]), 0) == cell, 1.0, 0.0).astype(bf16)


def scatter(values, ids, more=()):
    group, cell = ids >> 9, ids & (CELLS - 1)
    spread = jnp.concatenate([jnp.where(group == g, values, 0.0) for g in range(GROUPS)], axis=0)
    size = spread.shape[0]
    both = jnp.concatenate(split(spread) + tuple(more), axis=0)
    sums = lax.dot_general(both, hot(cell), (((1,), (1,)), ((), ())), preferred_element_type=f32)
    return sums[:size] + sums[size : 2 * size], sums[2 * size :]


def gather(parts, ids):
    group, cell = ids >> 9, ids & (CELLS - 1)
    size = parts[0].shape[0]
    found = jnp.dot(jnp.concatenate(parts, axis=0), hot(cell), preferred_element_type=f32)
    found = sum(found[size * i : size * (i + 1)] for i in range(1, len(parts))) + found[:size]
    part = size // GROUPS
    picked = jnp.where(group == 0, found[:part], 0.0)
    for g in range(1, GROUPS):
        picked = picked + jnp.where(group == g, found[g * part : (g + 1) * part], 0.0)
    return picked


def store_lines(lines_ref, array):
    cols = array.shape[1] // LANES
    for i in range(array.shape[0] // 8):
        for k in range(cols):
            start = 8 * (i * cols + k)
            lines_ref[start : start + 8, 0, :] = array[8 * i : 8 * i + 8, LANES * k : LANES * (k + 1)]


def load_lines(lines_ref, first, count):
    cols = 4
    return jnp.concatenate(
        [
            jnp.concatenate([lines_ref[8 * (i * cols + k) : 8 * (i * cols + k) + 8, 0, :] for k in range(cols)], axis=1)
            for i in range(first, first + count)
        ],
        axis=0,
    )


def store_tiles(tiles_ref, array, first=0):
    lines = tiles_ref.shape[1]
    rows, cols = array.shape[0] // lines, array.shape[1] // LANES
    for i in range(rows):
        for k in range(cols):
            tile = array[lines * i : lines * (i + 1), LANES * k : LANES * (k + 1)]
            tiles_ref[(first + i) * cols + k] = tile.astype(tiles_ref.dtype)


def load_tiles(tiles_ref, first, count):
    cols = 4
    return jnp.concatenate(
        [
            jnp.concatenate([tiles_ref[i * cols + k].astype(f32) for k in range(cols)], axis=1)
            for i in range(first, first + count)
        ],
        axis=0,
    )


def edge_kernel(features_hbm, ids_hbm, rows_ref, first_ref, last_ref, features_ref, ids_ref, done):
    fetches = [
        pltpu.make_async_copy(features_hbm, features_ref, done.at[0]),
        pltpu.make_async_copy(ids_hbm, ids_ref, done.at[1]),
    ]
    for fetch in fetches:
        fetch.start()
    for fetch in fetches:
        fetch.wait()
    features = features_ref[...].astype(f32)
    row = lax.broadcasted_iota(jnp.int32, (16, LANES), 0)
    rows = []
    for r in range(4):
        mine = features[:, r // 2, r % 2, :]
        rows_ref[r] = mine.astype(bf16)
        ids = ids_ref[r // 2, r % 2 : r % 2 + 1]
        marks = jnp.where(row == 0, ids >> 8, jnp.where(row == 1, ids & 255, jnp.where(row == 2, 1, 0)))
        rows.append(jnp.concatenate([mine, marks.astype(f32)], axis=0))
    first, last = edges(rows)
    first_ref[...] = first.astype(bf16)
    last_ref[...] = last.astype(bf16)


def embed_kernel(place, low, mid, high, taps_one, taps_two, bias, ids_ref, back_one, back_two, marks, *outs):
    wide_ref, hidden_ref, embed_ref, lines_ref = outs
    widen((low, mid, high), wide_ref)
    gz, gy, gx = place[0], place[1], place[2]
    at = lane((CHANNELS, WIDE))
    inside = (at < LANES) | ((at < LANES + 3) & (gx < place[6])) | ((at >= WIDE - 3) & (gx > 0))

    def layer(z, carry):
        for y in range(4):
            folded = fold(jnp.dot(taps_one[...], window(wide_ref, z, y), preferred_element_type=f32))
            folded = jnp.maximum(folded + bias[...], 0.0)
            depth, row = 2 * gz - 1 + z, 2 * gy - 1 + y
            exists = (depth >= 0) & (depth < 2 * place[4] + 2) & (row >= 0) & (row < 2 * place[5] + 2)
            hidden_ref[z, y] = jnp.where(inside & exists, folded, 0.0).astype(bf16)
        return carry

    lax.fori_loop(0, 4, layer, 0, unroll=True)
    pack = jnp.zeros((EMBED, LANES), f32)
    at = lane((EMBED, LANES))
    for r in range(4):
        folded = fold(jnp.dot(taps_two[...], window(hidden_ref, r // 2, r % 2), preferred_element_type=f32))
        embed_ref[:, LANES * r : LANES * (r + 1)] = folded[:, :LANES]
        edge = folded[:, LANES:] if r == 0 else pltpu.roll(folded[:, LANES:], 8 * r, 1)
        pack = jnp.where(((at - 8 * r + 4) & (LANES - 1)) < 8, edge, pack)
    embed_ref[:, ROW_COLS:] = pack
    ids = ids_ref[...]
    row = lax.broadcasted_iota(jnp.int32, (16, CELLS), 0)
    ones = jnp.where((ids >> 9) == row, 1.0, 0.0).astype(bf16)
    sums, counts = scatter(embed_ref[:, :ROW_COLS], ids, (ones,))
    store_lines(lines_ref, jnp.concatenate([sums, counts[:8]], axis=0))


def direct_kernel(place, lines_ref, embed_ref, ids_ref, pack_ref, direct_ref, sent_ref):
    centers, table = [], []
    row = lax.broadcasted_iota(jnp.int32, (16, CELLS), 0)
    counts = load_lines(lines_ref, 8, 1)
    for g in range(GROUPS):
        count = counts[g : g + 1]
        centers.append(load_lines(lines_ref, 2 * g, 2) / count)
        table += [centers[g], jnp.where(row == 0, 1.0 / count, 0.0)]
    pack = pack_ref[...].astype(f32)
    pack_ids = (256.0 * pack[0:1] + pack[1:2]).astype(jnp.int32)
    ids = jnp.concatenate([ids_ref[...], pack_ids], axis=1)
    mark = jnp.concatenate([jnp.ones((1, ROW_COLS), f32), pack[2:3]], axis=1)
    near = gather(split(jnp.concatenate(table, axis=0)), ids)
    share = near[EMBED : EMBED + 1] * mark
    offset = embed_ref[...] - near[:EMBED]
    hinge = jnp.maximum(jnp.sum(offset * offset, axis=0, keepdims=True) - pull_margin, 0.0)
    direct = (4.0 / SEGMENTS) * hinge * share * offset
    row = lax.broadcasted_iota(jnp.int32, (8, ids.shape[1]), 0)
    marks = jnp.where(row == 0, ids.astype(f32), jnp.where(row == 1, share, 0.0))
    direct_ref[...] = jnp.concatenate([direct, marks], axis=0)
    few = jnp.where(row == 0, (ids >> 8).astype(f32), jnp.where(row == 1, (ids & 255).astype(f32), 0.0))
    shares = split(share)
    few = jnp.where(row == 2, shares[0].astype(f32), jnp.where(row == 3, shares[1].astype(f32), few))
    for i, part in enumerate((direct[:8], direct[8:], few)):
        for k in range(5):
            sent_ref[5 * i + k, 2] = part[:, LANES * k : LANES * (k + 1)].astype(bf16)
    sent_ref[15, 2] = jnp.zeros((8, LANES), bf16)
    sums, _ = scatter(direct[:, :ROW_COLS], ids_ref[...])
    mine = lane((EMBED, CELLS)) == place[3]
    scale = 8.0 / (SEGMENTS * (SEGMENTS - 1.0))
    for g in range(GROUPS):
        own = jnp.sum(jnp.where(mine, centers[g], 0.0), axis=1, keepdims=True)
        total = jnp.zeros((EMBED, CELLS), f32)
        for other in centers:
            difference = own - other
            distance = jnp.sum(difference * difference, axis=0, keepdims=True)
            total = total + jnp.maximum(push_margin - distance, 0.0) * difference
        push = -scale * jnp.sum(total, axis=1, keepdims=True)
        grad = jnp.where(mine, push, 0.0) - sums[EMBED * g : EMBED * (g + 1)]
        for k in range(4):
            for half in range(2):
                part = grad[8 * half : 8 * half + 8, LANES * k : LANES * (k + 1)]
                sent_ref[4 * g + k, half] = part.astype(bf16)


def backward_layers(hidden_ref, up_ref, taps_two, grad_ref):
    def layer(z, carry):
        for y in range(4):
            folded = fold(jnp.dot(taps_two[...], window(up_ref, z, y), preferred_element_type=f32))
            grad_ref[z, y] = jnp.where(hidden_ref[z, y].astype(f32) > 0.0, folded, 0.0).astype(bf16)
        return carry

    lax.fori_loop(0, 4, layer, 0, unroll=True)


def kernels_kernel(direct_ref, got_ref, wide_ref, hidden_ref, taps_two, block_ref, sent_ref, up_ref, grad_ref):
    def tiles(first, count, which):
        return jnp.concatenate([got_ref[first + k, which].astype(f32) for k in range(count)], axis=1)

    table = jnp.concatenate([tiles(4 * g, 4, half) for g in range(GROUPS) for half in range(2)], axis=0).astype(bf16)
    for zb in range(3):
        if zb == 1:
            direct = direct_ref[:EMBED]
            ids = direct_ref[EMBED : EMBED + 1].astype(jnp.int32)
            share = direct_ref[EMBED + 1 : EMBED + 2]
        else:
            which = 2 + zb // 2
            direct = jnp.concatenate([tiles(0, 5, which), tiles(5, 5, which)], axis=0)
            few = tiles(10, 5, which)
            ids = (256.0 * few[0:1] + few[1:2]).astype(jnp.int32)
            share = few[2:3] + few[3:4]
        upstream = VOXELS * (direct + gather((table,), ids) * share)
        rounded = upstream.astype(bf16)
        for r in range(5):
            block_ref[zb, r] = rounded[:, LANES * r : LANES * (r + 1)]
            for half in range(2):
                part = upstream[8 * half : 8 * half + 8, LANES * r : LANES * (r + 1)]
                sent_ref[2 * (5 * zb + r) + half, 3] = part.astype(bf16)
    for n in range(30, 32):
        sent_ref[n, 3] = jnp.zeros((8, LANES), bf16)
    up_ref[...] = jnp.zeros(up_ref.shape, bf16)
    for r in range(4):
        up_ref[2 + r // 2, 2 + r % 2, :, 0:LANES] = block_ref[1, r]
    backward_layers(hidden_ref, up_ref, taps_two, grad_ref)
    over_cells = (((1,), (1,)), ((), ()))

    def shifted(row):
        row = row.astype(f32)
        return jnp.concatenate([pltpu.roll(row, WIDE - 1, 1), row, pltpu.roll(row, 1, 1)], axis=0).astype(bf16)

    def layer(z, carry):
        one, bias = carry
        moved = jnp.concatenate([shifted(grad_ref[z, y]) for y in range(4)], axis=1)
        seen = jnp.concatenate([window(wide_ref, z, y) for y in range(4)], axis=1)
        one = one + lax.dot_general(moved, seen, over_cells, preferred_element_type=f32)
        for y in range(4):
            bias = bias + grad_ref[z, y].astype(f32)
        return one, bias

    zeros = jnp.zeros((3 * CHANNELS, 9 * CHANNELS), f32), jnp.zeros((CHANNELS, WIDE), f32)
    one, bias = lax.fori_loop(0, 4, layer, zeros, unroll=True)
    ones = jnp.ones((16, 2 * WIDE), bf16)
    bias = jnp.concatenate(split(bias), axis=1)
    bias = lax.dot_general(ones, bias, over_cells, preferred_element_type=f32)
    moved = jnp.concatenate([shifted(up_ref[2 + r // 2, 2 + r % 2]) for r in range(4)], axis=1)
    seen = jnp.concatenate([window(hidden_ref, r // 2, r % 2) for r in range(4)], axis=1)
    two = lax.dot_general(seen, moved, over_cells, preferred_element_type=f32).T
    one = jnp.concatenate([one, jnp.zeros((3 * CHANNELS, 80), f32)], axis=1)
    bias = jnp.concatenate([bias] * 3, axis=0)
    two = jnp.concatenate([two, bias, jnp.zeros((3 * EMBED, 32), f32)], axis=1)
    whole = jnp.concatenate([one, two], axis=0)
    for i in range(8):
        for k in range(4):
            for j in range(3):
                part = whole[24 * i + 8 * j : 24 * i + 8 * j + 8, LANES * k : LANES * (k + 1)]
                sent_ref[4 * i + k, j] = part.astype(bf16)


def last_kernel(got_ref, mid, hidden_ref, taps_two, taps_one, *rest):
    features_ref, one_ref, bias_ref, two_ref, low, high, up_ref, grad_ref = rest
    for n in range(15):
        for which, ref in ((3, low), (4, high)):
            tile = [got_ref[2 * n + half, which].astype(f32) for half in range(2)]
            ref[n // 5, n % 5] = jnp.concatenate(tile, axis=0).astype(bf16)
    widen((low, mid, high), up_ref)
    backward_layers(hidden_ref, up_ref, taps_two, grad_ref)
    for r in range(4):
        folded = fold(jnp.dot(taps_one[...], window(grad_ref, r // 2, r % 2), preferred_element_type=f32))
        features_ref[:, r // 2, r % 2, :] = folded[:, :LANES].astype(bf16)
    whole = jnp.concatenate(
        [
            jnp.concatenate([got_ref[4 * i + k, j].astype(f32) for k in range(4)], axis=1)
            for i in range(8)
            for j in range(3)
        ],
        axis=0,
    ) * (1.0 / VOXELS)
    for c in range(3):
        part = whole[CHANNELS * c : CHANNELS * (c + 1)]
        for ab in range(9):
            one_ref[ab * 3 + c] = part[:, CHANNELS * ab : CHANNELS * (ab + 1)]
        part = whole[3 * CHANNELS + EMBED * c : 3 * CHANNELS + EMBED * (c + 1)]
        for ab in range(9):
            two_ref[ab * 3 + c] = part[:, CHANNELS * ab : CHANNELS * (ab + 1)]
    bias_ref[...] = whole[3 * CHANNELS : 3 * CHANNELS + 1, 9 * CHANNELS : 10 * CHANNELS]


def passed(low, high, axis):
    count = lax.axis_size(axis)
    forward = [(i, i + 1) for i in range(count - 1)]
    backward = [(target, source) for source, target in forward]
    return lax.ppermute(high, axis, forward), lax.ppermute(low, axis, backward)


def add_up(pieces):
    return jnp.sum(pieces.astype(f32), 0).astype(pieces.dtype)


def copies(piece, axes):
    return jnp.broadcast_to(piece[None], (lax.axis_size(axes),) + piece.shape)


def total(pieces, outer, inner):
    piece = add_up(lax.all_to_all(pieces, outer, 0, 0))
    piece = add_up(lax.all_to_all(copies(piece, inner), inner, 0, 0))
    return lax.all_to_all(copies(piece, outer), outer, 0, 0)


def total_and_relay(pieces, outer, inner, stride):
    held = lax.all_to_all(pieces, outer, 0, 0)
    piece = add_up(held[:, :-1])
    pieces = lax.all_to_all(copies(piece, inner), inner, 0, 0)
    pieces, held = lax.optimization_barrier((pieces, held))
    piece, block = add_up(pieces), held[:, -1:]
    none = jnp.zeros_like(block[:stride])
    low = jnp.concatenate([none, block[:-stride]], axis=0)
    high = jnp.concatenate([block[stride:], none], axis=0)
    return lax.all_to_all(jnp.concatenate([copies(piece, outer), low, high], axis=1), outer, 0, 0)


def shards(features, segment_ids, kernel_one, bias_one, kernel_two):
    axes = ("gz", "gy", "gx")
    place = jnp.stack(
        [lax.axis_index(axis) for axis in axes]
        + [lax.axis_index(axes)]
        + [jnp.int32(lax.axis_size(axis) - 1) for axis in axes]
    ).astype(jnp.int32)
    taps_one = jnp.transpose(kernel_one, (2, 3, 0, 1, 4)).reshape(3 * CHANNELS, 9 * CHANNELS)
    taps_two = jnp.transpose(kernel_two, (2, 3, 0, 1, 4)).reshape(3 * EMBED, 9 * CHANNELS)
    back_one = jnp.transpose(kernel_one[::-1, ::-1, ::-1], (2, 4, 0, 1, 3)).reshape(3 * CHANNELS, 9 * CHANNELS)
    back_two = jnp.transpose(kernel_two[::-1, ::-1, ::-1], (2, 4, 0, 1, 3)).reshape(3 * CHANNELS, 9 * EMBED)
    ids = segment_ids.reshape(1, ROW_COLS)

    rows, first, last = pl.pallas_call(
        edge_kernel,
        out_shape=[jax.ShapeDtypeStruct((4, CHANNELS, LANES), bf16)]
        + [jax.ShapeDtypeStruct((CHANNELS + 16, LANES), bf16)] * 2,
        in_specs=[pl.BlockSpec(memory_space=pl.ANY)] * 2,
        out_specs=[pl.BlockSpec(memory_space=pltpu.VMEM)] * 3,
        scratch_shapes=[
            pltpu.VMEM(features.shape, bf16),
            pltpu.VMEM(segment_ids.shape, jnp.int32),
            pltpu.SemaphoreType.DMA((2,)),
        ],
    )(features, segment_ids)
    left, right = passed(first, last, "gx")
    pack = left + right
    block = jnp.concatenate([rows, pack[None, :CHANNELS]], axis=0)
    low, high = passed(block, block, "gz")
    mid = jnp.stack([low, block, high])
    low, high = passed(mid, mid, "gy")
    marks = pack[CHANNELS:]
    wide, hidden, embedding, lines = kernel_call(
        embed_kernel,
        [
            ((6, 6, CHANNELS, WIDE), bf16),
            ((4, 4, CHANNELS, WIDE), bf16),
            ((EMBED, ROW_COLS + LANES), f32),
            ((288, 1, LANES), f32),
        ],
        scalars=1,
    )(place, low, mid, high, taps_one, taps_two, bias_one[:, None], ids, back_one, back_two, marks)
    lines = total(lines.reshape(32, 9, 1, LANES), ("gy", "gx"), "gz").reshape(lines.shape)
    direct, sent = kernel_call(
        direct_kernel, [((24, ROW_COLS + LANES), f32), ((16, 3, 8, LANES), bf16)], scalars=1
    )(place, lines, embedding, ids, marks)
    got = total_and_relay(sent, "gz", ("gy", "gx"), 1)
    back = [((6, 6, EMBED, WIDE), bf16), ((4, 4, CHANNELS, WIDE), bf16)]
    block = ((3, 5, EMBED, LANES), bf16)
    mid, sent = kernel_call(kernels_kernel, [block, ((32, 4, 8, LANES), bf16)], scratch=back)(
        direct, got, wide, hidden, back_two
    )
    got = total_and_relay(sent, ("gy", "gx"), "gz", lax.axis_size("gx"))
    grad_features, grad_one, grad_bias, grad_two = kernel_call(
        last_kernel,
        [
            ((CHANNELS, 2, 2, LANES), bf16),
            ((27, CHANNELS, CHANNELS), f32),
            ((1, CHANNELS), f32),
            ((27, EMBED, CHANNELS), f32),
        ],
        scratch=[block, block] + back,
    )(got, mid, hidden, back_two, back_one)
    return (
        grad_features,
        grad_one.reshape(3, 3, 3, CHANNELS, CHANNELS),
        grad_bias.reshape(CHANNELS),
        grad_two.reshape(3, 3, 3, EMBED, CHANNELS),
    )


def solution(mesh):
    return jax.shard_map(
        shards,
        mesh=mesh,
        in_specs=(P(None, "gz", "gy", "gx"), P("gz", "gy", "gx"), P(), P(), P()),
        out_specs=(P(None, "gz", "gy", "gx"), P(), P(), P()),
        check_vma=False,
    )
```

```python
import functools

import jax
import jax.numpy as jnp
from jax import lax
from jax.experimental import pallas as pl
from jax.experimental.pallas import tpu as pltpu
from jax.sharding import PartitionSpec as P

EMBED = 16
CHANNELS = 48
LANES = 128
WIDE = 2 * LANES
CELLS = 512
GROUPS = 4
ROW_COLS = 512
VOXELS = 262144.0
SEGMENTS = 2048.0
pull_margin = 4.0
push_margin = 8.0
f32, bf16 = jnp.float32, jnp.bfloat16


def kernel_call(body, outs, scratch=(), scalars=0, flops=0):
    def call(*args):
        specs = [pl.BlockSpec(memory_space=pltpu.SMEM)] * scalars
        specs += [pl.BlockSpec(memory_space=pltpu.VMEM)] * (len(args) - scalars)
        return pl.pallas_call(
            body,
            out_shape=[jax.ShapeDtypeStruct(shape, dtype) for shape, dtype in outs],
            in_specs=specs,
            out_specs=[pl.BlockSpec(memory_space=pltpu.VMEM)] * len(outs),
            scratch_shapes=[pltpu.VMEM(shape, dtype) for shape, dtype in scratch],
            compiler_params=pltpu.CompilerParams(vmem_limit_bytes=40 * 1024 * 1024),
        )(*args)

    return call


def lane(shape):
    return lax.broadcasted_iota(jnp.int32, shape, len(shape) - 1)


def edges(rows):
    at = lane(rows[0].shape)
    first = jnp.zeros(rows[0].shape, f32)
    last = jnp.zeros(rows[0].shape, f32)
    for r, row in enumerate(rows):
        turned = row if r == 0 else pltpu.roll(row, 8 * r, 1)
        first = jnp.where((at >= 8 * r) & (at < 8 * r + 4), turned, first)
        start = (8 * r - 4) % LANES
        last = jnp.where((at >= start) & (at < start + 4), turned, last)
    return first, last


def widen(blocks, wide_ref):
    for yb, ref in enumerate(blocks):
        for zb in range(3):
            pack = ref[zb, 4].astype(f32)
            for r in range(4):
                edge = pack if r == 0 else pltpu.roll(pack, LANES - 8 * r, 1)
                z, y = 2 * zb + r // 2, 2 * yb + r % 2
                wide_ref[z, y, :, 0:LANES] = ref[zb, r]
                wide_ref[z, y, :, LANES:WIDE] = edge.astype(bf16)


def window(ref, z, y):
    size = ref.shape[2]
    return jnp.concatenate([ref[z + a, y : y + 3].reshape(3 * size, WIDE) for a in range(3)], axis=0)


def fold(taps):
    size = taps.shape[0] // 3
    return pltpu.roll(taps[:size], 1, 1) + taps[size : 2 * size] + pltpu.roll(taps[2 * size :], WIDE - 1, 1)


def split(value, count):
    parts = []
    for _ in range(count):
        parts.append(value.astype(bf16))
        value = value - parts[-1].astype(f32)
    return tuple(parts)


def hot(cell):
    return jnp.where(lax.broadcasted_iota(jnp.int32, (CELLS, cell.shape[1]), 0) == cell, 1.0, 0.0).astype(bf16)


def scatter(values, ids, count, more=()):
    group, cell = ids >> 9, ids & (CELLS - 1)
    spread = jnp.concatenate([jnp.where(group == g, values, 0.0) for g in range(GROUPS)], axis=0)
    size = spread.shape[0]
    parts = jnp.concatenate(split(spread, count) + tuple(more), axis=0)
    sums = lax.dot_general(parts, hot(cell), (((1,), (1,)), ((), ())), preferred_element_type=f32)
    found = sum(sums[size * i : size * (i + 1)] for i in range(1, count)) + sums[:size]
    return found, sums[count * size :]


def gather(parts, ids):
    group, cell = ids >> 9, ids & (CELLS - 1)
    size = parts[0].shape[0]
    found = jnp.dot(jnp.concatenate(parts, axis=0), hot(cell), preferred_element_type=f32)
    found = sum(found[size * i : size * (i + 1)] for i in range(1, len(parts))) + found[:size]
    part = size // GROUPS
    picked = jnp.where(group == 0, found[:part], 0.0)
    for g in range(1, GROUPS):
        picked = picked + jnp.where(group == g, found[g * part : (g + 1) * part], 0.0)
    return picked


def store_lines(lines_ref, array):
    cols = array.shape[1] // LANES
    for i in range(array.shape[0] // 8):
        for k in range(cols):
            start = 8 * (i * cols + k)
            lines_ref[start : start + 8, 0, :] = array[8 * i : 8 * i + 8, LANES * k : LANES * (k + 1)]


def load_lines(lines_ref, first, count):
    cols = 4
    return jnp.concatenate(
        [
            jnp.concatenate([lines_ref[8 * (i * cols + k) : 8 * (i * cols + k) + 8, 0, :] for k in range(cols)], axis=1)
            for i in range(first, first + count)
        ],
        axis=0,
    )


def store_tiles(tiles_ref, array, first=0):
    lines = tiles_ref.shape[1]
    rows, cols = array.shape[0] // lines, array.shape[1] // LANES
    for i in range(rows):
        for k in range(cols):
            tile = array[lines * i : lines * (i + 1), LANES * k : LANES * (k + 1)]
            tiles_ref[(first + i) * cols + k] = tile.astype(tiles_ref.dtype)


def load_tiles(tiles_ref, first, count):
    cols = 4
    return jnp.concatenate(
        [
            jnp.concatenate([tiles_ref[i * cols + k].astype(f32) for k in range(cols)], axis=1)
            for i in range(first, first + count)
        ],
        axis=0,
    )


def edge_kernel(features_hbm, ids_hbm, first_ref, last_ref, features_ref, ids_ref, done):
    fetches = [
        pltpu.make_async_copy(features_hbm, features_ref, done.at[0]),
        pltpu.make_async_copy(ids_hbm, ids_ref, done.at[1]),
    ]
    for fetch in fetches:
        fetch.start()
    for fetch in fetches:
        fetch.wait()
    features = features_ref[...].astype(f32)
    row = lax.broadcasted_iota(jnp.int32, (16, LANES), 0)
    rows = []
    for r in range(4):
        mine = features[:, r // 2, r % 2, :]
        ids = ids_ref[r // 2, r % 2 : r % 2 + 1]
        marks = jnp.where(row == 0, ids >> 8, jnp.where(row == 1, ids & 255, jnp.where(row == 2, 1, 0)))
        rows.append(jnp.concatenate([mine, marks.astype(f32)], axis=0))
    first, last = edges(rows)
    first_ref[...] = first.astype(bf16)
    last_ref[...] = last.astype(bf16)


def embed_kernel(place, low, mid, high, taps_one, taps_two, bias, ids_ref, back_one, back_two, marks, *outs):
    wide_ref, hidden_ref, embed_ref, lines_ref = outs
    widen((low, mid, high), wide_ref)
    gz, gy, gx = place[0], place[1], place[2]
    at = lane((CHANNELS, WIDE))
    inside = (at < LANES) | ((at < LANES + 3) & (gx < place[6])) | ((at >= WIDE - 3) & (gx > 0))

    def layer(z, carry):
        for y in range(4):
            folded = fold(jnp.dot(taps_one[...], window(wide_ref, z, y), preferred_element_type=f32))
            folded = jnp.maximum(folded + bias[...], 0.0)
            depth, row = 2 * gz - 1 + z, 2 * gy - 1 + y
            exists = (depth >= 0) & (depth < 2 * place[4] + 2) & (row >= 0) & (row < 2 * place[5] + 2)
            hidden_ref[z, y] = jnp.where(inside & exists, folded, 0.0).astype(bf16)
        return carry

    lax.fori_loop(0, 4, layer, 0, unroll=True)
    pack = jnp.zeros((EMBED, LANES), f32)
    at = lane((EMBED, LANES))
    for r in range(4):
        folded = fold(jnp.dot(taps_two[...], window(hidden_ref, r // 2, r % 2), preferred_element_type=f32))
        embed_ref[:, LANES * r : LANES * (r + 1)] = folded[:, :LANES]
        edge = folded[:, LANES:] if r == 0 else pltpu.roll(folded[:, LANES:], 8 * r, 1)
        pack = jnp.where(((at - 8 * r + 4) & (LANES - 1)) < 8, edge, pack)
    embed_ref[:, ROW_COLS:] = pack
    ids = ids_ref[...]
    row = lax.broadcasted_iota(jnp.int32, (16, CELLS), 0)
    ones = jnp.where((ids >> 9) == row, 1.0, 0.0).astype(bf16)
    sums, counts = scatter(embed_ref[:, :ROW_COLS], ids, 3, (ones,))
    store_lines(lines_ref, jnp.concatenate([sums, counts[:8]], axis=0))


def direct_kernel(place, lines_ref, embed_ref, ids_ref, pack_ref, direct_ref, sent_ref):
    centers, table = [], []
    row = lax.broadcasted_iota(jnp.int32, (16, CELLS), 0)
    counts = load_lines(lines_ref, 8, 1)
    for g in range(GROUPS):
        count = counts[g : g + 1]
        centers.append(load_lines(lines_ref, 2 * g, 2) / count)
        table += [centers[g], jnp.where(row == 0, 1.0 / count, 0.0)]
    pack = pack_ref[...].astype(f32)
    pack_ids = (256.0 * pack[0:1] + pack[1:2]).astype(jnp.int32)
    ids = jnp.concatenate([ids_ref[...], pack_ids], axis=1)
    mark = jnp.concatenate([jnp.ones((1, ROW_COLS), f32), pack[2:3]], axis=1)
    near = gather(split(jnp.concatenate(table, axis=0), 3), ids)
    share = near[EMBED : EMBED + 1] * mark
    offset = embed_ref[...] - near[:EMBED]
    hinge = jnp.maximum(jnp.sum(offset * offset, axis=0, keepdims=True) - pull_margin, 0.0)
    direct = (4.0 / SEGMENTS) * hinge * share * offset
    row = lax.broadcasted_iota(jnp.int32, (8, ids.shape[1]), 0)
    marks = jnp.where(row == 0, ids.astype(f32), jnp.where(row == 1, share, 0.0))
    direct_ref[...] = jnp.concatenate([direct, marks], axis=0)
    few = jnp.where(row == 0, (ids >> 8).astype(f32), jnp.where(row == 1, (ids & 255).astype(f32), 0.0))
    shares = split(share, 2)
    few = jnp.where(row == 2, shares[0].astype(f32), jnp.where(row == 3, shares[1].astype(f32), few))
    for i, part in enumerate((direct[:8], direct[8:], few)):
        for k in range(5):
            sent_ref[5 * i + k, 2] = part[:, LANES * k : LANES * (k + 1)].astype(bf16)
    sent_ref[15, 2] = jnp.zeros((8, LANES), bf16)
    sums, _ = scatter(direct[:, :ROW_COLS], ids_ref[...], 2)
    mine = lane((EMBED, CELLS)) == place[3]
    scale = 8.0 / (SEGMENTS * (SEGMENTS - 1.0))
    for g in range(GROUPS):
        own = jnp.sum(jnp.where(mine, centers[g], 0.0), axis=1, keepdims=True)
        total = jnp.zeros((EMBED, CELLS), f32)
        for other in centers:
            difference = own - other
            distance = jnp.sum(difference * difference, axis=0, keepdims=True)
            total = total + jnp.maximum(push_margin - distance, 0.0) * difference
        push = -scale * jnp.sum(total, axis=1, keepdims=True)
        grad = jnp.where(mine, push, 0.0) - sums[EMBED * g : EMBED * (g + 1)]
        for k in range(4):
            for half in range(2):
                part = grad[8 * half : 8 * half + 8, LANES * k : LANES * (k + 1)]
                sent_ref[4 * g + k, half] = part.astype(bf16)


def backward_layers(hidden_ref, up_ref, taps_two, grad_ref):
    def layer(z, carry):
        for y in range(4):
            folded = fold(jnp.dot(taps_two[...], window(up_ref, z, y), preferred_element_type=f32))
            grad_ref[z, y] = jnp.where(hidden_ref[z, y].astype(f32) > 0.0, folded, 0.0).astype(bf16)
        return carry

    lax.fori_loop(0, 4, layer, 0, unroll=True)


def kernels_kernel(direct_ref, got_ref, wide_ref, hidden_ref, taps_two, block_ref, sent_ref, up_ref, grad_ref):
    def tiles(first, count, which):
        return jnp.concatenate([got_ref[first + k, which].astype(f32) for k in range(count)], axis=1)

    table = jnp.concatenate([tiles(4 * g, 4, half) for g in range(GROUPS) for half in range(2)], axis=0).astype(bf16)
    for zb in range(3):
        if zb == 1:
            direct = direct_ref[:EMBED]
            ids = direct_ref[EMBED : EMBED + 1].astype(jnp.int32)
            share = direct_ref[EMBED + 1 : EMBED + 2]
        else:
            which = 2 + zb // 2
            direct = jnp.concatenate([tiles(0, 5, which), tiles(5, 5, which)], axis=0)
            few = tiles(10, 5, which)
            ids = (256.0 * few[0:1] + few[1:2]).astype(jnp.int32)
            share = few[2:3] + few[3:4]
        upstream = VOXELS * (direct + gather((table,), ids) * share)
        rounded = upstream.astype(bf16)
        for r in range(5):
            block_ref[zb, r] = rounded[:, LANES * r : LANES * (r + 1)]
            for half in range(2):
                part = upstream[8 * half : 8 * half + 8, LANES * r : LANES * (r + 1)]
                sent_ref[2 * (5 * zb + r) + half, 3] = part.astype(bf16)
    for n in range(30, 32):
        sent_ref[n, 3] = jnp.zeros((8, LANES), bf16)
    up_ref[...] = jnp.zeros(up_ref.shape, bf16)
    for r in range(4):
        up_ref[2 + r // 2, 2 + r % 2, :, 0:LANES] = block_ref[1, r]
    backward_layers(hidden_ref, up_ref, taps_two, grad_ref)
    over_cells = (((1,), (1,)), ((), ()))

    def shifted(row):
        row = row.astype(f32)
        return jnp.concatenate([pltpu.roll(row, WIDE - 1, 1), row, pltpu.roll(row, 1, 1)], axis=0).astype(bf16)

    def layer(z, carry):
        one, bias = carry
        moved = jnp.concatenate([shifted(grad_ref[z, y]) for y in range(4)], axis=1)
        seen = jnp.concatenate([window(wide_ref, z, y) for y in range(4)], axis=1)
        one = one + lax.dot_general(moved, seen, over_cells, preferred_element_type=f32)
        for y in range(4):
            bias = bias + grad_ref[z, y].astype(f32)
        return one, bias

    zeros = jnp.zeros((3 * CHANNELS, 9 * CHANNELS), f32), jnp.zeros((CHANNELS, WIDE), f32)
    one, bias = lax.fori_loop(0, 4, layer, zeros, unroll=True)
    ones = jnp.ones((16, 2 * WIDE), bf16)
    bias = jnp.concatenate(split(bias, 2), axis=1)
    bias = lax.dot_general(ones, bias, over_cells, preferred_element_type=f32)
    moved = jnp.concatenate([shifted(up_ref[2 + r // 2, 2 + r % 2]) for r in range(4)], axis=1)
    seen = jnp.concatenate([window(hidden_ref, r // 2, r % 2) for r in range(4)], axis=1)
    two = lax.dot_general(seen, moved, over_cells, preferred_element_type=f32).T
    one = jnp.concatenate([one, jnp.zeros((3 * CHANNELS, 80), f32)], axis=1)
    bias = jnp.concatenate([bias] * 3, axis=0)
    two = jnp.concatenate([two, bias, jnp.zeros((3 * EMBED, 32), f32)], axis=1)
    whole = jnp.concatenate([one, two], axis=0)
    for i in range(8):
        for k in range(4):
            for j in range(3):
                part = whole[24 * i + 8 * j : 24 * i + 8 * j + 8, LANES * k : LANES * (k + 1)]
                sent_ref[4 * i + k, j] = part.astype(bf16)


def last_kernel(got_ref, mid, hidden_ref, taps_two, taps_one, *rest):
    features_ref, one_ref, bias_ref, two_ref, low, high, up_ref, grad_ref = rest
    for n in range(15):
        for which, ref in ((3, low), (4, high)):
            tile = [got_ref[2 * n + half, which].astype(f32) for half in range(2)]
            ref[n // 5, n % 5] = jnp.concatenate(tile, axis=0).astype(bf16)
    widen((low, mid, high), up_ref)
    backward_layers(hidden_ref, up_ref, taps_two, grad_ref)
    for r in range(4):
        folded = fold(jnp.dot(taps_one[...], window(grad_ref, r // 2, r % 2), preferred_element_type=f32))
        features_ref[:, r // 2, r % 2, :] = folded[:, :LANES].astype(bf16)
    whole = jnp.concatenate(
        [
            jnp.concatenate([got_ref[4 * i + k, j].astype(f32) for k in range(4)], axis=1)
            for i in range(8)
            for j in range(3)
        ],
        axis=0,
    ) * (1.0 / VOXELS)
    for c in range(3):
        part = whole[CHANNELS * c : CHANNELS * (c + 1)]
        for ab in range(9):
            one_ref[ab * 3 + c] = part[:, CHANNELS * ab : CHANNELS * (ab + 1)]
        part = whole[3 * CHANNELS + EMBED * c : 3 * CHANNELS + EMBED * (c + 1)]
        for ab in range(9):
            two_ref[ab * 3 + c] = part[:, CHANNELS * ab : CHANNELS * (ab + 1)]
    bias_ref[...] = whole[3 * CHANNELS : 3 * CHANNELS + 1, 9 * CHANNELS : 10 * CHANNELS]


def passed(low, high, axis):
    count = lax.axis_size(axis)
    forward = [(i, i + 1) for i in range(count - 1)]
    backward = [(target, source) for source, target in forward]
    return lax.ppermute(high, axis, forward), lax.ppermute(low, axis, backward)


def add_up(pieces):
    return jnp.sum(pieces.astype(f32), 0).astype(pieces.dtype)


def copies(piece, axes):
    return jnp.broadcast_to(piece[None], (lax.axis_size(axes),) + piece.shape)


def total(pieces, outer, inner):
    piece = add_up(lax.all_to_all(pieces, outer, 0, 0))
    piece = add_up(lax.all_to_all(copies(piece, inner), inner, 0, 0))
    return lax.all_to_all(copies(piece, outer), outer, 0, 0)


def total_and_relay(pieces, outer, inner, stride):
    held = lax.all_to_all(pieces, outer, 0, 0)
    piece = add_up(held[:, :-1])
    pieces = lax.all_to_all(copies(piece, inner), inner, 0, 0)
    pieces, held = lax.optimization_barrier((pieces, held))
    piece, block = add_up(pieces), held[:, -1:]
    none = jnp.zeros_like(block[:stride])
    low = jnp.concatenate([none, block[:-stride]], axis=0)
    high = jnp.concatenate([block[stride:], none], axis=0)
    return lax.all_to_all(jnp.concatenate([copies(piece, outer), low, high], axis=1), outer, 0, 0)


def shards(features, segment_ids, kernel_one, bias_one, kernel_two):
    axes = ("gz", "gy", "gx")
    place = jnp.stack(
        [lax.axis_index(axis) for axis in axes]
        + [lax.axis_index(axes)]
        + [jnp.int32(lax.axis_size(axis) - 1) for axis in axes]
    ).astype(jnp.int32)
    taps_one = jnp.transpose(kernel_one, (2, 3, 0, 1, 4)).reshape(3 * CHANNELS, 9 * CHANNELS)
    taps_two = jnp.transpose(kernel_two, (2, 3, 0, 1, 4)).reshape(3 * EMBED, 9 * CHANNELS)
    back_one = jnp.transpose(kernel_one[::-1, ::-1, ::-1], (2, 4, 0, 1, 3)).reshape(3 * CHANNELS, 9 * CHANNELS)
    back_two = jnp.transpose(kernel_two[::-1, ::-1, ::-1], (2, 4, 0, 1, 3)).reshape(3 * CHANNELS, 9 * EMBED)
    ids = segment_ids.reshape(1, ROW_COLS)

    first, last = pl.pallas_call(
        edge_kernel,
        out_shape=[jax.ShapeDtypeStruct((CHANNELS + 16, LANES), bf16)] * 2,
        in_specs=[pl.BlockSpec(memory_space=pl.ANY)] * 2,
        out_specs=[pl.BlockSpec(memory_space=pltpu.VMEM)] * 2,
        scratch_shapes=[
            pltpu.VMEM(features.shape, bf16),
            pltpu.VMEM(segment_ids.shape, jnp.int32),
            pltpu.SemaphoreType.DMA((2,)),
        ],
    )(features, segment_ids)
    rows = jnp.transpose(features, (1, 2, 0, 3)).reshape(4, CHANNELS, LANES)
    left, right = passed(first, last, "gx")
    pack = left + right
    block = jnp.concatenate([rows, pack[None, :CHANNELS]], axis=0)
    low, high = passed(block, block, "gz")
    mid = jnp.stack([low, block, high])
    low, high = passed(mid, mid, "gy")
    marks = pack[CHANNELS:]
    wide, hidden, embedding, lines = kernel_call(
        embed_kernel,
        [
            ((6, 6, CHANNELS, WIDE), bf16),
            ((4, 4, CHANNELS, WIDE), bf16),
            ((EMBED, ROW_COLS + LANES), f32),
            ((288, 1, LANES), f32),
        ],
        scalars=1,
    )(place, low, mid, high, taps_one, taps_two, bias_one[:, None], ids, back_one, back_two, marks)
    lines = total(lines.reshape(32, 9, 1, LANES), ("gy", "gx"), "gz").reshape(lines.shape)
    direct, sent = kernel_call(
        direct_kernel, [((24, ROW_COLS + LANES), f32), ((16, 3, 8, LANES), bf16)], scalars=1
    )(place, lines, embedding, ids, marks)
    got = total_and_relay(sent, "gz", ("gy", "gx"), 1)
    back = [((6, 6, EMBED, WIDE), bf16), ((4, 4, CHANNELS, WIDE), bf16)]
    block = ((3, 5, EMBED, LANES), bf16)
    mid, sent = kernel_call(kernels_kernel, [block, ((32, 4, 8, LANES), bf16)], scratch=back)(
        direct, got, wide, hidden, back_two
    )
    got = total_and_relay(sent, ("gy", "gx"), "gz", lax.axis_size("gx"))
    grad_features, grad_one, grad_bias, grad_two = kernel_call(
        last_kernel,
        [
            ((CHANNELS, 2, 2, LANES), bf16),
            ((27, CHANNELS, CHANNELS), f32),
            ((1, CHANNELS), f32),
            ((27, EMBED, CHANNELS), f32),
        ],
        scratch=[block, block] + back,
    )(got, mid, hidden, back_two, back_one)
    return (
        grad_features,
        grad_one.reshape(3, 3, 3, CHANNELS, CHANNELS),
        grad_bias.reshape(CHANNELS),
        grad_two.reshape(3, 3, 3, EMBED, CHANNELS),
    )


def solution(mesh):
    return jax.shard_map(
        shards,
        mesh=mesh,
        in_specs=(P(None, "gz", "gy", "gx"), P("gz", "gy", "gx"), P(), P(), P()),
        out_specs=(P(None, "gz", "gy", "gx"), P(), P(), P()),
        check_vma=False,
    )
```

```python
import functools

import jax
import jax.numpy as jnp
from jax import lax
from jax.experimental import pallas as pl
from jax.experimental.pallas import tpu as pltpu
from jax.sharding import PartitionSpec as P

EMBED = 16
CHANNELS = 48
LANES = 128
WIDE = 2 * LANES
CELLS = 512
GROUPS = 4
ROW_COLS = 512
VOXELS = 262144.0
SEGMENTS = 2048.0
pull_margin = 4.0
push_margin = 8.0
f32, bf16 = jnp.float32, jnp.bfloat16


def kernel_call(body, outs, scratch=(), scalars=0, flops=0):
    def call(*args):
        specs = [pl.BlockSpec(memory_space=pltpu.SMEM)] * scalars
        specs += [pl.BlockSpec(memory_space=pltpu.VMEM)] * (len(args) - scalars)
        return pl.pallas_call(
            body,
            out_shape=[jax.ShapeDtypeStruct(shape, dtype) for shape, dtype in outs],
            in_specs=specs,
            out_specs=[pl.BlockSpec(memory_space=pltpu.VMEM)] * len(outs),
            scratch_shapes=[pltpu.VMEM(shape, dtype) for shape, dtype in scratch],
            compiler_params=pltpu.CompilerParams(vmem_limit_bytes=40 * 1024 * 1024),
        )(*args)

    return call


def lane(shape):
    return lax.broadcasted_iota(jnp.int32, shape, len(shape) - 1)


def edges(rows):
    at = lane(rows[0].shape)
    first = jnp.zeros(rows[0].shape, f32)
    last = jnp.zeros(rows[0].shape, f32)
    for r, row in enumerate(rows):
        turned = row if r == 0 else pltpu.roll(row, 8 * r, 1)
        first = jnp.where((at >= 8 * r) & (at < 8 * r + 4), turned, first)
        start = (8 * r - 4) % LANES
        last = jnp.where((at >= start) & (at < start + 4), turned, last)
    return first, last


def widen(blocks, wide_ref):
    for yb, ref in enumerate(blocks):
        for zb in range(3):
            pack = ref[zb, 4].astype(f32)
            for r in range(4):
                edge = pack if r == 0 else pltpu.roll(pack, LANES - 8 * r, 1)
                z, y = 2 * zb + r // 2, 2 * yb + r % 2
                wide_ref[z, y, :, 0:LANES] = ref[zb, r]
                wide_ref[z, y, :, LANES:WIDE] = edge.astype(bf16)


def window(ref, z, y):
    size = ref.shape[2]
    return jnp.concatenate([ref[z + a, y : y + 3].reshape(3 * size, WIDE) for a in range(3)], axis=0)


def fold(taps):
    size = taps.shape[0] // 3
    return pltpu.roll(taps[:size], 1, 1) + taps[size : 2 * size] + pltpu.roll(taps[2 * size :], WIDE - 1, 1)


def split(value, count):
    parts = []
    for _ in range(count):
        parts.append(value.astype(bf16))
        value = value - parts[-1].astype(f32)
    return tuple(parts)


def hot(cell):
    return jnp.where(lax.broadcasted_iota(jnp.int32, (CELLS, cell.shape[1]), 0) == cell, 1.0, 0.0).astype(bf16)


def scatter(values, ids, count, more=()):
    group, cell = ids >> 9, ids & (CELLS - 1)
    spread = jnp.concatenate([jnp.where(group == g, values, 0.0) for g in range(GROUPS)], axis=0)
    size = spread.shape[0]
    parts = jnp.concatenate(split(spread, count) + tuple(more), axis=0)
    sums = lax.dot_general(parts, hot(cell), (((1,), (1,)), ((), ())), preferred_element_type=f32)
    found = sum(sums[size * i : size * (i + 1)] for i in range(1, count)) + sums[:size]
    return found, sums[count * size :]


def gather(parts, ids):
    group, cell = ids >> 9, ids & (CELLS - 1)
    size = parts[0].shape[0]
    found = jnp.dot(jnp.concatenate(parts, axis=0), hot(cell), preferred_element_type=f32)
    found = sum(found[size * i : size * (i + 1)] for i in range(1, len(parts))) + found[:size]
    part = size // GROUPS
    picked = jnp.where(group == 0, found[:part], 0.0)
    for g in range(1, GROUPS):
        picked = picked + jnp.where(group == g, found[g * part : (g + 1) * part], 0.0)
    return picked


def store_lines(lines_ref, array):
    cols = array.shape[1] // LANES
    for i in range(array.shape[0] // 8):
        for k in range(cols):
            start = 8 * (i * cols + k)
            lines_ref[start : start + 8, 0, :] = array[8 * i : 8 * i + 8, LANES * k : LANES * (k + 1)]


def load_lines(lines_ref, first, count):
    cols = 4
    return jnp.concatenate(
        [
            jnp.concatenate([lines_ref[8 * (i * cols + k) : 8 * (i * cols + k) + 8, 0, :] for k in range(cols)], axis=1)
            for i in range(first, first + count)
        ],
        axis=0,
    )


def store_tiles(tiles_ref, array, first=0):
    lines = tiles_ref.shape[1]
    rows, cols = array.shape[0] // lines, array.shape[1] // LANES
    for i in range(rows):
        for k in range(cols):
            tile = array[lines * i : lines * (i + 1), LANES * k : LANES * (k + 1)]
            tiles_ref[(first + i) * cols + k] = tile.astype(tiles_ref.dtype)


def load_tiles(tiles_ref, first, count):
    cols = 4
    return jnp.concatenate(
        [
            jnp.concatenate([tiles_ref[i * cols + k].astype(f32) for k in range(cols)], axis=1)
            for i in range(first, first + count)
        ],
        axis=0,
    )


def edge_kernel(features_hbm, ids_hbm, sent_ref, features_ref, ids_ref, done):
    fetches = [
        pltpu.make_async_copy(features_hbm, features_ref, done.at[0]),
        pltpu.make_async_copy(ids_hbm, ids_ref, done.at[1]),
    ]
    for fetch in fetches:
        fetch.start()
    row = lax.broadcasted_iota(jnp.int32, (16, LANES), 0)
    fetches[1].wait()
    marked = []
    for r in range(4):
        ids = ids_ref[r // 2, r % 2 : r % 2 + 1]
        marks = jnp.where(row == 0, ids >> 8, jnp.where(row == 1, ids & 255, jnp.where(row == 2, 1, 0)))
        marked.append(marks.astype(f32))
    fetches[0].wait()
    features = features_ref[...].astype(f32)
    rows = []
    for r in range(4):
        mine = features[:, r // 2, r % 2, :]
        rows.append(jnp.concatenate([mine, marked[r]], axis=0))
    first, last = edges(rows)
    gx = lax.axis_index("gx")
    first, last = first.astype(bf16), last.astype(bf16)
    sent_ref[...] = jnp.zeros(sent_ref.shape, bf16)

    @pl.when(gx > 0)
    def _():
        sent_ref[jnp.maximum(gx - 1, 0)] = first

    @pl.when(gx < sent_ref.shape[0] - 1)
    def _():
        sent_ref[jnp.minimum(gx + 1, sent_ref.shape[0] - 1)] = last


def embed_kernel(place, low, mid, high, taps_one, taps_two, bias, ids_ref, back_one, back_two, marks, *outs):
    wide_ref, hidden_ref, embed_ref, lines_ref = outs
    widen((low, mid, high), wide_ref)
    gz, gy, gx = place[0], place[1], place[2]
    at = lane((CHANNELS, WIDE))
    inside = (at < LANES) | ((at < LANES + 3) & (gx < place[6])) | ((at >= WIDE - 3) & (gx > 0))

    def layer(z, carry):
        for y in range(4):
            folded = fold(jnp.dot(taps_one[...], window(wide_ref, z, y), preferred_element_type=f32))
            folded = jnp.maximum(folded + bias[...], 0.0)
            depth, row = 2 * gz - 1 + z, 2 * gy - 1 + y
            exists = (depth >= 0) & (depth < 2 * place[4] + 2) & (row >= 0) & (row < 2 * place[5] + 2)
            hidden_ref[z, y] = jnp.where(inside & exists, folded, 0.0).astype(bf16)
        return carry

    lax.fori_loop(0, 4, layer, 0, unroll=True)
    pack = jnp.zeros((EMBED, LANES), f32)
    at = lane((EMBED, LANES))
    for r in range(4):
        folded = fold(jnp.dot(taps_two[...], window(hidden_ref, r // 2, r % 2), preferred_element_type=f32))
        embed_ref[:, LANES * r : LANES * (r + 1)] = folded[:, :LANES]
        edge = folded[:, LANES:] if r == 0 else pltpu.roll(folded[:, LANES:], 8 * r, 1)
        pack = jnp.where(((at - 8 * r + 4) & (LANES - 1)) < 8, edge, pack)
    embed_ref[:, ROW_COLS:] = pack
    ids = ids_ref[...]
    row = lax.broadcasted_iota(jnp.int32, (16, CELLS), 0)
    ones = jnp.where((ids >> 9) == row, 1.0, 0.0).astype(bf16)
    sums, counts = scatter(embed_ref[:, :ROW_COLS], ids, 3, (ones,))
    store_lines(lines_ref, jnp.concatenate([sums, counts[:8]], axis=0))


def direct_kernel(place, lines_ref, embed_ref, ids_ref, pack_ref, direct_ref, sent_ref):
    centers, table = [], []
    row = lax.broadcasted_iota(jnp.int32, (16, CELLS), 0)
    counts = load_lines(lines_ref, 8, 1)
    for g in range(GROUPS):
        count = counts[g : g + 1]
        centers.append(load_lines(lines_ref, 2 * g, 2) / count)
        table += [centers[g], jnp.where(row == 0, 1.0 / count, 0.0)]
    pack = pack_ref[...].astype(f32)
    pack_ids = (256.0 * pack[0:1] + pack[1:2]).astype(jnp.int32)
    ids = jnp.concatenate([ids_ref[...], pack_ids], axis=1)
    mark = jnp.concatenate([jnp.ones((1, ROW_COLS), f32), pack[2:3]], axis=1)
    near = gather(split(jnp.concatenate(table, axis=0), 3), ids)
    share = near[EMBED : EMBED + 1] * mark
    offset = embed_ref[...] - near[:EMBED]
    hinge = jnp.maximum(jnp.sum(offset * offset, axis=0, keepdims=True) - pull_margin, 0.0)
    direct = (4.0 / SEGMENTS) * hinge * share * offset
    row = lax.broadcasted_iota(jnp.int32, (8, ids.shape[1]), 0)
    marks = jnp.where(row == 0, ids.astype(f32), jnp.where(row == 1, share, 0.0))
    direct_ref[...] = jnp.concatenate([direct, marks], axis=0)
    few = jnp.where(row == 0, (ids >> 8).astype(f32), jnp.where(row == 1, (ids & 255).astype(f32), 0.0))
    shares = split(share, 2)
    few = jnp.where(row == 2, shares[0].astype(f32), jnp.where(row == 3, shares[1].astype(f32), few))
    for i, part in enumerate((direct[:8], direct[8:], few)):
        for k in range(5):
            sent_ref[5 * i + k, 2] = part[:, LANES * k : LANES * (k + 1)].astype(bf16)
    sent_ref[15, 2] = jnp.zeros((8, LANES), bf16)
    sums, _ = scatter(direct[:, :ROW_COLS], ids_ref[...], 2)
    mine = lane((EMBED, CELLS)) == place[3]
    scale = 8.0 / (SEGMENTS * (SEGMENTS - 1.0))
    for g in range(GROUPS):
        own = jnp.sum(jnp.where(mine, centers[g], 0.0), axis=1, keepdims=True)
        total = jnp.zeros((EMBED, CELLS), f32)
        for other in centers:
            difference = own - other
            distance = jnp.sum(difference * difference, axis=0, keepdims=True)
            total = total + jnp.maximum(push_margin - distance, 0.0) * difference
        push = -scale * jnp.sum(total, axis=1, keepdims=True)
        grad = jnp.where(mine, push, 0.0) - sums[EMBED * g : EMBED * (g + 1)]
        for k in range(4):
            for half in range(2):
                part = grad[8 * half : 8 * half + 8, LANES * k : LANES * (k + 1)]
                sent_ref[4 * g + k, half] = part.astype(bf16)


def backward_layers(hidden_ref, up_ref, taps_two, grad_ref):
    def layer(z, carry):
        for y in range(4):
            folded = fold(jnp.dot(taps_two[...], window(up_ref, z, y), preferred_element_type=f32))
            grad_ref[z, y] = jnp.where(hidden_ref[z, y].astype(f32) > 0.0, folded, 0.0).astype(bf16)
        return carry

    lax.fori_loop(0, 4, layer, 0, unroll=True)


def kernels_kernel(direct_ref, got_ref, wide_ref, hidden_ref, taps_two, block_ref, sent_ref, up_ref, grad_ref):
    def tiles(first, count, which):
        return jnp.concatenate([got_ref[first + k, which].astype(f32) for k in range(count)], axis=1)

    table = jnp.concatenate([tiles(4 * g, 4, half) for g in range(GROUPS) for half in range(2)], axis=0).astype(bf16)
    for zb in range(3):
        if zb == 1:
            direct = direct_ref[:EMBED]
            ids = direct_ref[EMBED : EMBED + 1].astype(jnp.int32)
            share = direct_ref[EMBED + 1 : EMBED + 2]
        else:
            which = 2 + zb // 2
            direct = jnp.concatenate([tiles(0, 5, which), tiles(5, 5, which)], axis=0)
            few = tiles(10, 5, which)
            ids = (256.0 * few[0:1] + few[1:2]).astype(jnp.int32)
            share = few[2:3] + few[3:4]
        upstream = VOXELS * (direct + gather((table,), ids) * share)
        rounded = upstream.astype(bf16)
        for r in range(5):
            block_ref[zb, r] = rounded[:, LANES * r : LANES * (r + 1)]
            for half in range(2):
                part = upstream[8 * half : 8 * half + 8, LANES * r : LANES * (r + 1)]
                sent_ref[2 * (5 * zb + r) + half, 3] = part.astype(bf16)
    for n in range(30, 32):
        sent_ref[n, 3] = jnp.zeros((8, LANES), bf16)
    up_ref[...] = jnp.zeros(up_ref.shape, bf16)
    for r in range(4):
        up_ref[2 + r // 2, 2 + r % 2, :, 0:LANES] = block_ref[1, r]
    backward_layers(hidden_ref, up_ref, taps_two, grad_ref)
    over_cells = (((1,), (1,)), ((), ()))

    def shifted(row):
        row = row.astype(f32)
        return jnp.concatenate([pltpu.roll(row, WIDE - 1, 1), row, pltpu.roll(row, 1, 1)], axis=0).astype(bf16)

    def layer(z, carry):
        one, bias = carry
        moved = jnp.concatenate([shifted(grad_ref[z, y]) for y in range(4)], axis=1)
        seen = jnp.concatenate([window(wide_ref, z, y) for y in range(4)], axis=1)
        one = one + lax.dot_general(moved, seen, over_cells, preferred_element_type=f32)
        for y in range(4):
            bias = bias + grad_ref[z, y].astype(f32)
        return one, bias

    zeros = jnp.zeros((3 * CHANNELS, 9 * CHANNELS), f32), jnp.zeros((CHANNELS, WIDE), f32)
    one, bias = lax.fori_loop(0, 4, layer, zeros, unroll=True)
    ones = jnp.ones((16, 2 * WIDE), bf16)
    bias = jnp.concatenate(split(bias, 2), axis=1)
    bias = lax.dot_general(ones, bias, over_cells, preferred_element_type=f32)
    moved = jnp.concatenate([shifted(up_ref[2 + r // 2, 2 + r % 2]) for r in range(4)], axis=1)
    seen = jnp.concatenate([window(hidden_ref, r // 2, r % 2) for r in range(4)], axis=1)
    two = lax.dot_general(seen, moved, over_cells, preferred_element_type=f32).T
    one = jnp.concatenate([one, jnp.zeros((3 * CHANNELS, 80), f32)], axis=1)
    bias = jnp.concatenate([bias] * 3, axis=0)
    two = jnp.concatenate([two, bias, jnp.zeros((3 * EMBED, 32), f32)], axis=1)
    whole = jnp.concatenate([one, two], axis=0)
    for i in range(8):
        for k in range(4):
            for j in range(3):
                part = whole[24 * i + 8 * j : 24 * i + 8 * j + 8, LANES * k : LANES * (k + 1)]
                sent_ref[4 * i + k, j] = part.astype(bf16)


def last_kernel(got_ref, mid, hidden_ref, taps_two, taps_one, *rest):
    features_ref, one_ref, bias_ref, two_ref, low, high, up_ref, grad_ref = rest
    for n in range(15):
        for which, ref in ((3, low), (4, high)):
            tile = [got_ref[2 * n + half, which].astype(f32) for half in range(2)]
            ref[n // 5, n % 5] = jnp.concatenate(tile, axis=0).astype(bf16)
    widen((low, mid, high), up_ref)
    backward_layers(hidden_ref, up_ref, taps_two, grad_ref)
    for r in range(4):
        folded = fold(jnp.dot(taps_one[...], window(grad_ref, r // 2, r % 2), preferred_element_type=f32))
        features_ref[:, r // 2, r % 2, :] = folded[:, :LANES].astype(bf16)
    whole = jnp.concatenate(
        [
            jnp.concatenate([got_ref[4 * i + k, j].astype(f32) for k in range(4)], axis=1)
            for i in range(8)
            for j in range(3)
        ],
        axis=0,
    ) * (1.0 / VOXELS)
    for c in range(3):
        part = whole[CHANNELS * c : CHANNELS * (c + 1)]
        for ab in range(9):
            one_ref[ab * 3 + c] = part[:, CHANNELS * ab : CHANNELS * (ab + 1)]
        part = whole[3 * CHANNELS + EMBED * c : 3 * CHANNELS + EMBED * (c + 1)]
        for ab in range(9):
            two_ref[ab * 3 + c] = part[:, CHANNELS * ab : CHANNELS * (ab + 1)]
    bias_ref[...] = whole[3 * CHANNELS : 3 * CHANNELS + 1, 9 * CHANNELS : 10 * CHANNELS]


def passed(low, high, axis):
    count = lax.axis_size(axis)
    forward = [(i, i + 1) for i in range(count - 1)]
    backward = [(target, source) for source, target in forward]
    return lax.ppermute(high, axis, forward), lax.ppermute(low, axis, backward)


def add_up(pieces):
    return jnp.sum(pieces.astype(f32), 0).astype(pieces.dtype)


def copies(piece, axes):
    return jnp.broadcast_to(piece[None], (lax.axis_size(axes),) + piece.shape)


def total(pieces, outer, inner):
    piece = add_up(lax.all_to_all(pieces, outer, 0, 0))
    piece = add_up(lax.all_to_all(copies(piece, inner), inner, 0, 0))
    return lax.all_to_all(copies(piece, outer), outer, 0, 0)


def total_and_relay(pieces, outer, inner, stride):
    held = lax.all_to_all(pieces, outer, 0, 0)
    piece = add_up(held[:, :-1])
    pieces = lax.all_to_all(copies(piece, inner), inner, 0, 0)
    pieces, held = lax.optimization_barrier((pieces, held))
    piece, block = add_up(pieces), held[:, -1:]
    none = jnp.zeros_like(block[:stride])
    low = jnp.concatenate([none, block[:-stride]], axis=0)
    high = jnp.concatenate([block[stride:], none], axis=0)
    return lax.all_to_all(jnp.concatenate([copies(piece, outer), low, high], axis=1), outer, 0, 0)


def shards(features, segment_ids, kernel_one, bias_one, kernel_two):
    axes = ("gz", "gy", "gx")
    place = jnp.stack(
        [lax.axis_index(axis) for axis in axes]
        + [lax.axis_index(axes)]
        + [jnp.int32(lax.axis_size(axis) - 1) for axis in axes]
    ).astype(jnp.int32)
    taps_one = jnp.transpose(kernel_one, (2, 3, 0, 1, 4)).reshape(3 * CHANNELS, 9 * CHANNELS)
    taps_two = jnp.transpose(kernel_two, (2, 3, 0, 1, 4)).reshape(3 * EMBED, 9 * CHANNELS)
    back_one = jnp.transpose(kernel_one[::-1, ::-1, ::-1], (2, 4, 0, 1, 3)).reshape(3 * CHANNELS, 9 * CHANNELS)
    back_two = jnp.transpose(kernel_two[::-1, ::-1, ::-1], (2, 4, 0, 1, 3)).reshape(3 * CHANNELS, 9 * EMBED)
    ids = segment_ids.reshape(1, ROW_COLS)

    sent = pl.pallas_call(
        edge_kernel,
        out_shape=jax.ShapeDtypeStruct((lax.axis_size("gx"), CHANNELS + 16, LANES), bf16),
        in_specs=[pl.BlockSpec(memory_space=pl.ANY)] * 2,
        out_specs=pl.BlockSpec(memory_space=pltpu.VMEM),
        scratch_shapes=[
            pltpu.VMEM(features.shape, bf16),
            pltpu.VMEM(segment_ids.shape, jnp.int32),
            pltpu.SemaphoreType.DMA((2,)),
        ],
    )(features, segment_ids)
    rows = jnp.transpose(features, (1, 2, 0, 3)).reshape(4, CHANNELS, LANES)
    pack = add_up(lax.all_to_all(sent, "gx", 0, 0))
    block = jnp.concatenate([rows, pack[None, :CHANNELS]], axis=0)
    low, high = passed(block, block, "gz")
    mid = jnp.stack([low, block, high])
    low, high = passed(mid, mid, "gy")
    marks = pack[CHANNELS:]
    wide, hidden, embedding, lines = kernel_call(
        embed_kernel,
        [
            ((6, 6, CHANNELS, WIDE), bf16),
            ((4, 4, CHANNELS, WIDE), bf16),
            ((EMBED, ROW_COLS + LANES), f32),
            ((288, 1, LANES), f32),
        ],
        scalars=1,
    )(place, low, mid, high, taps_one, taps_two, bias_one[:, None], ids, back_one, back_two, marks)
    lines = total(lines.reshape(32, 9, 1, LANES), ("gy", "gx"), "gz").reshape(lines.shape)
    direct, sent = kernel_call(
        direct_kernel, [((24, ROW_COLS + LANES), f32), ((16, 3, 8, LANES), bf16)], scalars=1
    )(place, lines, embedding, ids, marks)
    got = total_and_relay(sent, "gz", ("gy", "gx"), 1)
    back = [((6, 6, EMBED, WIDE), bf16), ((4, 4, CHANNELS, WIDE), bf16)]
    block = ((3, 5, EMBED, LANES), bf16)
    mid, sent = kernel_call(kernels_kernel, [block, ((32, 4, 8, LANES), bf16)], scratch=back)(
        direct, got, wide, hidden, back_two
    )
    got = total_and_relay(sent, ("gy", "gx"), "gz", lax.axis_size("gx"))
    grad_features, grad_one, grad_bias, grad_two = kernel_call(
        last_kernel,
        [
            ((CHANNELS, 2, 2, LANES), bf16),
            ((27, CHANNELS, CHANNELS), f32),
            ((1, CHANNELS), f32),
            ((27, EMBED, CHANNELS), f32),
        ],
        scratch=[block, block] + back,
    )(got, mid, hidden, back_two, back_one)
    return (
        grad_features,
        grad_one.reshape(3, 3, 3, CHANNELS, CHANNELS),
        grad_bias.reshape(CHANNELS),
        grad_two.reshape(3, 3, 3, EMBED, CHANNELS),
    )


def solution(mesh):
    return jax.shard_map(
        shards,
        mesh=mesh,
        in_specs=(P(None, "gz", "gy", "gx"), P("gz", "gy", "gx"), P(), P(), P()),
        out_specs=(P(None, "gz", "gy", "gx"), P(), P(), P()),
        check_vma=False,
    )
```

```python
import functools

import jax
import jax.numpy as jnp
from jax import lax
from jax.experimental import pallas as pl
from jax.experimental.pallas import tpu as pltpu
from jax.sharding import PartitionSpec as P

EMBED = 16
CHANNELS = 48
LANES = 128
WIDE = 2 * LANES
CELLS = 512
GROUPS = 4
ROW_COLS = 512
VOXELS = 262144.0
SEGMENTS = 2048.0
pull_margin = 4.0
push_margin = 8.0
f32, bf16 = jnp.float32, jnp.bfloat16


def kernel_call(body, outs, scratch=(), scalars=0, flops=0):
    def call(*args):
        specs = [pl.BlockSpec(memory_space=pltpu.SMEM)] * scalars
        specs += [pl.BlockSpec(memory_space=pltpu.VMEM)] * (len(args) - scalars)
        return pl.pallas_call(
            body,
            out_shape=[jax.ShapeDtypeStruct(shape, dtype) for shape, dtype in outs],
            in_specs=specs,
            out_specs=[pl.BlockSpec(memory_space=pltpu.VMEM)] * len(outs),
            scratch_shapes=[pltpu.VMEM(shape, dtype) for shape, dtype in scratch],
            compiler_params=pltpu.CompilerParams(vmem_limit_bytes=40 * 1024 * 1024),
        )(*args)

    return call


def lane(shape):
    return lax.broadcasted_iota(jnp.int32, shape, len(shape) - 1)


def edges(rows):
    at = lane(rows[0].shape)
    first = jnp.zeros(rows[0].shape, f32)
    last = jnp.zeros(rows[0].shape, f32)
    for r, row in enumerate(rows):
        turned = row if r == 0 else pltpu.roll(row, 8 * r, 1)
        first = jnp.where((at >= 8 * r) & (at < 8 * r + 4), turned, first)
        start = (8 * r - 4) % LANES
        last = jnp.where((at >= start) & (at < start + 4), turned, last)
    return first, last


def widen(blocks, wide_ref, by_depth=False):
    for yb, ref in enumerate(blocks):
        for zb in range(3):
            pack = ref[zb, 4].astype(f32)
            for r in range(4):
                edge = pack if r == 0 else pltpu.roll(pack, LANES - 8 * r, 1)
                z, y = (yb, zb) if by_depth else (zb, yb)
                z, y = 2 * z + r // 2, 2 * y + r % 2
                wide_ref[z, y, :, 0:LANES] = ref[zb, r]
                wide_ref[z, y, :, LANES:WIDE] = edge.astype(bf16)


def window(ref, z, y):
    size = ref.shape[2]
    return jnp.concatenate([ref[z + a, y : y + 3].reshape(3 * size, WIDE) for a in range(3)], axis=0)


def fold(taps):
    size = taps.shape[0] // 3
    return pltpu.roll(taps[:size], 1, 1) + taps[size : 2 * size] + pltpu.roll(taps[2 * size :], WIDE - 1, 1)


def split(value, count):
    parts = []
    for _ in range(count):
        parts.append(value.astype(bf16))
        value = value - parts[-1].astype(f32)
    return tuple(parts)


def hot(cell):
    return jnp.where(lax.broadcasted_iota(jnp.int32, (CELLS, cell.shape[1]), 0) == cell, 1.0, 0.0).astype(bf16)


def scatter(values, ids, count, more=()):
    group, cell = ids >> 9, ids & (CELLS - 1)
    spread = jnp.concatenate([jnp.where(group == g, values, 0.0) for g in range(GROUPS)], axis=0)
    size = spread.shape[0]
    parts = jnp.concatenate(split(spread, count) + tuple(more), axis=0)
    sums = lax.dot_general(parts, hot(cell), (((1,), (1,)), ((), ())), preferred_element_type=f32)
    found = sum(sums[size * i : size * (i + 1)] for i in range(1, count)) + sums[:size]
    return found, sums[count * size :]


def gather(parts, ids):
    group, cell = ids >> 9, ids & (CELLS - 1)
    size = parts[0].shape[0]
    found = jnp.dot(jnp.concatenate(parts, axis=0), hot(cell), preferred_element_type=f32)
    found = sum(found[size * i : size * (i + 1)] for i in range(1, len(parts))) + found[:size]
    part = size // GROUPS
    picked = jnp.where(group == 0, found[:part], 0.0)
    for g in range(1, GROUPS):
        picked = picked + jnp.where(group == g, found[g * part : (g + 1) * part], 0.0)
    return picked


def store_lines(lines_ref, array):
    cols = array.shape[1] // LANES
    for i in range(array.shape[0] // 8):
        for k in range(cols):
            start = 8 * (i * cols + k)
            lines_ref[start : start + 8, 0, :] = array[8 * i : 8 * i + 8, LANES * k : LANES * (k + 1)]


def load_lines(lines_ref, first, count):
    cols = 4
    return jnp.concatenate(
        [
            jnp.concatenate([lines_ref[8 * (i * cols + k) : 8 * (i * cols + k) + 8, 0, :] for k in range(cols)], axis=1)
            for i in range(first, first + count)
        ],
        axis=0,
    )


def store_tiles(tiles_ref, array, first=0):
    lines = tiles_ref.shape[1]
    rows, cols = array.shape[0] // lines, array.shape[1] // LANES
    for i in range(rows):
        for k in range(cols):
            tile = array[lines * i : lines * (i + 1), LANES * k : LANES * (k + 1)]
            tiles_ref[(first + i) * cols + k] = tile.astype(tiles_ref.dtype)


def load_tiles(tiles_ref, first, count):
    cols = 4
    return jnp.concatenate(
        [
            jnp.concatenate([tiles_ref[i * cols + k].astype(f32) for k in range(cols)], axis=1)
            for i in range(first, first + count)
        ],
        axis=0,
    )


def edge_kernel(features_hbm, ids_hbm, sent_ref, features_ref, ids_ref, done):
    fetches = [
        pltpu.make_async_copy(features_hbm, features_ref, done.at[0]),
        pltpu.make_async_copy(ids_hbm, ids_ref, done.at[1]),
    ]
    for fetch in fetches:
        fetch.start()
    row = lax.broadcasted_iota(jnp.int32, (16, LANES), 0)
    fetches[1].wait()
    marked = []
    for r in range(4):
        ids = ids_ref[r // 2, r % 2 : r % 2 + 1]
        marks = jnp.where(row == 0, ids >> 8, jnp.where(row == 1, ids & 255, jnp.where(row == 2, 1, 0)))
        marked.append(marks.astype(f32))
    fetches[0].wait()
    features = features_ref[...].astype(f32)
    rows = []
    for r in range(4):
        mine = features[:, r // 2, r % 2, :]
        rows.append(jnp.concatenate([mine, marked[r]], axis=0))
    first, last = edges(rows)
    gx = lax.axis_index("gx")
    first, last = first.astype(bf16), last.astype(bf16)
    sent_ref[...] = jnp.zeros(sent_ref.shape, bf16)

    @pl.when(gx > 0)
    def _():
        sent_ref[jnp.maximum(gx - 1, 0)] = first

    @pl.when(gx < sent_ref.shape[0] - 1)
    def _():
        sent_ref[jnp.minimum(gx + 1, sent_ref.shape[0] - 1)] = last


def embed_kernel(place, low, mid, high, taps_one, taps_two, bias, ids_ref, back_one, back_two, marks, *outs):
    wide_ref, hidden_ref, embed_ref, lines_ref = outs
    widen((low, mid, high), wide_ref, by_depth=True)
    gz, gy, gx = place[0], place[1], place[2]
    at = lane((CHANNELS, WIDE))
    inside = (at < LANES) | ((at < LANES + 3) & (gx < place[6])) | ((at >= WIDE - 3) & (gx > 0))

    def layer(z, carry):
        for y in range(4):
            folded = fold(jnp.dot(taps_one[...], window(wide_ref, z, y), preferred_element_type=f32))
            folded = jnp.maximum(folded + bias[...], 0.0)
            depth, row = 2 * gz - 1 + z, 2 * gy - 1 + y
            exists = (depth >= 0) & (depth < 2 * place[4] + 2) & (row >= 0) & (row < 2 * place[5] + 2)
            hidden_ref[z, y] = jnp.where(inside & exists, folded, 0.0).astype(bf16)
        return carry

    lax.fori_loop(0, 4, layer, 0, unroll=True)
    pack = jnp.zeros((EMBED, LANES), f32)
    at = lane((EMBED, LANES))
    for r in range(4):
        folded = fold(jnp.dot(taps_two[...], window(hidden_ref, r // 2, r % 2), preferred_element_type=f32))
        embed_ref[:, LANES * r : LANES * (r + 1)] = folded[:, :LANES]
        edge = folded[:, LANES:] if r == 0 else pltpu.roll(folded[:, LANES:], 8 * r, 1)
        pack = jnp.where(((at - 8 * r + 4) & (LANES - 1)) < 8, edge, pack)
    embed_ref[:, ROW_COLS:] = pack
    ids = ids_ref[...]
    row = lax.broadcasted_iota(jnp.int32, (16, CELLS), 0)
    ones = jnp.where((ids >> 9) == row, 1.0, 0.0).astype(bf16)
    sums, counts = scatter(embed_ref[:, :ROW_COLS], ids, 3, (ones,))
    store_lines(lines_ref, jnp.concatenate([sums, counts[:8]], axis=0))


def direct_kernel(place, lines_ref, embed_ref, ids_ref, pack_ref, direct_ref, sent_ref):
    centers, table = [], []
    row = lax.broadcasted_iota(jnp.int32, (16, CELLS), 0)
    counts = load_lines(lines_ref, 8, 1)
    for g in range(GROUPS):
        count = counts[g : g + 1]
        centers.append(load_lines(lines_ref, 2 * g, 2) / count)
        table += [centers[g], jnp.where(row == 0, 1.0 / count, 0.0)]
    pack = pack_ref[...].astype(f32)
    pack_ids = (256.0 * pack[0:1] + pack[1:2]).astype(jnp.int32)
    ids = jnp.concatenate([ids_ref[...], pack_ids], axis=1)
    mark = jnp.concatenate([jnp.ones((1, ROW_COLS), f32), pack[2:3]], axis=1)
    near = gather(split(jnp.concatenate(table, axis=0), 3), ids)
    share = near[EMBED : EMBED + 1] * mark
    offset = embed_ref[...] - near[:EMBED]
    hinge = jnp.maximum(jnp.sum(offset * offset, axis=0, keepdims=True) - pull_margin, 0.0)
    direct = (4.0 / SEGMENTS) * hinge * share * offset
    row = lax.broadcasted_iota(jnp.int32, (8, ids.shape[1]), 0)
    marks = jnp.where(row == 0, ids.astype(f32), jnp.where(row == 1, share, 0.0))
    direct_ref[...] = jnp.concatenate([direct, marks], axis=0)
    few = jnp.where(row == 0, (ids >> 8).astype(f32), jnp.where(row == 1, (ids & 255).astype(f32), 0.0))
    shares = split(share, 2)
    few = jnp.where(row == 2, shares[0].astype(f32), jnp.where(row == 3, shares[1].astype(f32), few))
    for i, part in enumerate((direct[:8], direct[8:], few)):
        for k in range(5):
            sent_ref[5 * i + k, 2] = part[:, LANES * k : LANES * (k + 1)].astype(bf16)
    sent_ref[15, 2] = jnp.zeros((8, LANES), bf16)
    sums, _ = scatter(direct[:, :ROW_COLS], ids_ref[...], 2)
    mine = lane((EMBED, CELLS)) == place[3]
    scale = 8.0 / (SEGMENTS * (SEGMENTS - 1.0))
    for g in range(GROUPS):
        own = jnp.sum(jnp.where(mine, centers[g], 0.0), axis=1, keepdims=True)
        total = jnp.zeros((EMBED, CELLS), f32)
        for other in centers:
            difference = own - other
            distance = jnp.sum(difference * difference, axis=0, keepdims=True)
            total = total + jnp.maximum(push_margin - distance, 0.0) * difference
        push = -scale * jnp.sum(total, axis=1, keepdims=True)
        grad = jnp.where(mine, push, 0.0) - sums[EMBED * g : EMBED * (g + 1)]
        for k in range(4):
            for half in range(2):
                part = grad[8 * half : 8 * half + 8, LANES * k : LANES * (k + 1)]
                sent_ref[4 * g + k, half] = part.astype(bf16)


def backward_layers(hidden_ref, up_ref, taps_two, grad_ref):
    def layer(z, carry):
        for y in range(4):
            folded = fold(jnp.dot(taps_two[...], window(up_ref, z, y), preferred_element_type=f32))
            grad_ref[z, y] = jnp.where(hidden_ref[z, y].astype(f32) > 0.0, folded, 0.0).astype(bf16)
        return carry

    lax.fori_loop(0, 4, layer, 0, unroll=True)


def kernels_kernel(direct_ref, got_ref, wide_ref, hidden_ref, taps_two, block_ref, sent_ref, up_ref, grad_ref):
    def tiles(first, count, which):
        return jnp.concatenate([got_ref[first + k, which].astype(f32) for k in range(count)], axis=1)

    table = jnp.concatenate([tiles(4 * g, 4, half) for g in range(GROUPS) for half in range(2)], axis=0).astype(bf16)
    for zb in range(3):
        if zb == 1:
            direct = direct_ref[:EMBED]
            ids = direct_ref[EMBED : EMBED + 1].astype(jnp.int32)
            share = direct_ref[EMBED + 1 : EMBED + 2]
        else:
            which = 2 + zb // 2
            direct = jnp.concatenate([tiles(0, 5, which), tiles(5, 5, which)], axis=0)
            few = tiles(10, 5, which)
            ids = (256.0 * few[0:1] + few[1:2]).astype(jnp.int32)
            share = few[2:3] + few[3:4]
        upstream = VOXELS * (direct + gather((table,), ids) * share)
        rounded = upstream.astype(bf16)
        for r in range(5):
            block_ref[zb, r] = rounded[:, LANES * r : LANES * (r + 1)]
            for half in range(2):
                part = upstream[8 * half : 8 * half + 8, LANES * r : LANES * (r + 1)]
                sent_ref[2 * (5 * zb + r) + half, 3] = part.astype(bf16)
    for n in range(30, 32):
        sent_ref[n, 3] = jnp.zeros((8, LANES), bf16)
    up_ref[...] = jnp.zeros(up_ref.shape, bf16)
    for r in range(4):
        up_ref[2 + r // 2, 2 + r % 2, :, 0:LANES] = block_ref[1, r]
    backward_layers(hidden_ref, up_ref, taps_two, grad_ref)
    over_cells = (((1,), (1,)), ((), ()))

    def shifted(row):
        row = row.astype(f32)
        return jnp.concatenate([pltpu.roll(row, WIDE - 1, 1), row, pltpu.roll(row, 1, 1)], axis=0).astype(bf16)

    def layer(z, carry):
        one, bias = carry
        moved = jnp.concatenate([shifted(grad_ref[z, y]) for y in range(4)], axis=1)
        seen = jnp.concatenate([window(wide_ref, z, y) for y in range(4)], axis=1)
        one = one + lax.dot_general(moved, seen, over_cells, preferred_element_type=f32)
        for y in range(4):
            bias = bias + grad_ref[z, y].astype(f32)
        return one, bias

    zeros = jnp.zeros((3 * CHANNELS, 9 * CHANNELS), f32), jnp.zeros((CHANNELS, WIDE), f32)
    one, bias = lax.fori_loop(0, 4, layer, zeros, unroll=True)
    ones = jnp.ones((16, 2 * WIDE), bf16)
    bias = jnp.concatenate(split(bias, 2), axis=1)
    bias = lax.dot_general(ones, bias, over_cells, preferred_element_type=f32)
    moved = jnp.concatenate([shifted(up_ref[2 + r // 2, 2 + r % 2]) for r in range(4)], axis=1)
    seen = jnp.concatenate([window(hidden_ref, r // 2, r % 2) for r in range(4)], axis=1)
    two = lax.dot_general(seen, moved, over_cells, preferred_element_type=f32).T
    one = jnp.concatenate([one, jnp.zeros((3 * CHANNELS, 80), f32)], axis=1)
    bias = jnp.concatenate([bias] * 3, axis=0)
    two = jnp.concatenate([two, bias, jnp.zeros((3 * EMBED, 32), f32)], axis=1)
    whole = jnp.concatenate([one, two], axis=0)
    for i in range(8):
        for k in range(4):
            for j in range(3):
                part = whole[24 * i + 8 * j : 24 * i + 8 * j + 8, LANES * k : LANES * (k + 1)]
                sent_ref[4 * i + k, j] = part.astype(bf16)


def last_kernel(got_ref, mid, hidden_ref, taps_two, taps_one, *rest):
    features_ref, one_ref, bias_ref, two_ref, low, high, up_ref, grad_ref = rest
    for n in range(15):
        for which, ref in ((3, low), (4, high)):
            tile = [got_ref[2 * n + half, which].astype(f32) for half in range(2)]
            ref[n // 5, n % 5] = jnp.concatenate(tile, axis=0).astype(bf16)
    widen((low, mid, high), up_ref)
    backward_layers(hidden_ref, up_ref, taps_two, grad_ref)
    for r in range(4):
        folded = fold(jnp.dot(taps_one[...], window(grad_ref, r // 2, r % 2), preferred_element_type=f32))
        features_ref[:, r // 2, r % 2, :] = folded[:, :LANES].astype(bf16)
    whole = jnp.concatenate(
        [
            jnp.concatenate([got_ref[4 * i + k, j].astype(f32) for k in range(4)], axis=1)
            for i in range(8)
            for j in range(3)
        ],
        axis=0,
    ) * (1.0 / VOXELS)
    for c in range(3):
        part = whole[CHANNELS * c : CHANNELS * (c + 1)]
        for ab in range(9):
            one_ref[ab * 3 + c] = part[:, CHANNELS * ab : CHANNELS * (ab + 1)]
        part = whole[3 * CHANNELS + EMBED * c : 3 * CHANNELS + EMBED * (c + 1)]
        for ab in range(9):
            two_ref[ab * 3 + c] = part[:, CHANNELS * ab : CHANNELS * (ab + 1)]
    bias_ref[...] = whole[3 * CHANNELS : 3 * CHANNELS + 1, 9 * CHANNELS : 10 * CHANNELS]


def passed(low, high, axis):
    count = lax.axis_size(axis)
    forward = [(i, i + 1) for i in range(count - 1)]
    backward = [(target, source) for source, target in forward]
    return lax.ppermute(high, axis, forward), lax.ppermute(low, axis, backward)


def add_up(pieces):
    return jnp.sum(pieces.astype(f32), 0).astype(pieces.dtype)


def copies(piece, axes):
    return jnp.broadcast_to(piece[None], (lax.axis_size(axes),) + piece.shape)


def total(pieces, outer, inner):
    piece = add_up(lax.all_to_all(pieces, outer, 0, 0))
    piece = add_up(lax.all_to_all(copies(piece, inner), inner, 0, 0))
    return lax.all_to_all(copies(piece, outer), outer, 0, 0)


def total_and_relay(pieces, outer, inner, stride):
    held = lax.all_to_all(pieces, outer, 0, 0)
    piece = add_up(held[:, :-1])
    pieces = lax.all_to_all(copies(piece, inner), inner, 0, 0)
    pieces, held = lax.optimization_barrier((pieces, held))
    piece, block = add_up(pieces), held[:, -1:]
    none = jnp.zeros_like(block[:stride])
    low = jnp.concatenate([none, block[:-stride]], axis=0)
    high = jnp.concatenate([block[stride:], none], axis=0)
    return lax.all_to_all(jnp.concatenate([copies(piece, outer), low, high], axis=1), outer, 0, 0)


def shards(features, segment_ids, kernel_one, bias_one, kernel_two):
    axes = ("gz", "gy", "gx")
    place = jnp.stack(
        [lax.axis_index(axis) for axis in axes]
        + [lax.axis_index(axes)]
        + [jnp.int32(lax.axis_size(axis) - 1) for axis in axes]
    ).astype(jnp.int32)
    taps_one = jnp.transpose(kernel_one, (2, 3, 0, 1, 4)).reshape(3 * CHANNELS, 9 * CHANNELS)
    taps_two = jnp.transpose(kernel_two, (2, 3, 0, 1, 4)).reshape(3 * EMBED, 9 * CHANNELS)
    back_one = jnp.transpose(kernel_one[::-1, ::-1, ::-1], (2, 4, 0, 1, 3)).reshape(3 * CHANNELS, 9 * CHANNELS)
    back_two = jnp.transpose(kernel_two[::-1, ::-1, ::-1], (2, 4, 0, 1, 3)).reshape(3 * CHANNELS, 9 * EMBED)
    ids = segment_ids.reshape(1, ROW_COLS)

    sent = pl.pallas_call(
        edge_kernel,
        out_shape=jax.ShapeDtypeStruct((lax.axis_size("gx"), CHANNELS + 16, LANES), bf16),
        in_specs=[pl.BlockSpec(memory_space=pl.ANY)] * 2,
        out_specs=pl.BlockSpec(memory_space=pltpu.VMEM),
        scratch_shapes=[
            pltpu.VMEM(features.shape, bf16),
            pltpu.VMEM(segment_ids.shape, jnp.int32),
            pltpu.SemaphoreType.DMA((2,)),
        ],
    )(features, segment_ids)
    rows = jnp.transpose(features, (1, 2, 0, 3)).reshape(4, CHANNELS, LANES)
    pack = add_up(lax.all_to_all(sent, "gx", 0, 0))
    block = jnp.concatenate([rows, pack[None, :CHANNELS]], axis=0)
    low, high = passed(block, block, "gy")
    mid = jnp.stack([low, block, high])
    low, high = passed(mid, mid, "gz")
    marks = pack[CHANNELS:]
    wide, hidden, embedding, lines = kernel_call(
        embed_kernel,
        [
            ((6, 6, CHANNELS, WIDE), bf16),
            ((4, 4, CHANNELS, WIDE), bf16),
            ((EMBED, ROW_COLS + LANES), f32),
            ((288, 1, LANES), f32),
        ],
        scalars=1,
    )(place, low, mid, high, taps_one, taps_two, bias_one[:, None], ids, back_one, back_two, marks)
    lines = total(lines.reshape(32, 9, 1, LANES), ("gy", "gx"), "gz").reshape(lines.shape)
    direct, sent = kernel_call(
        direct_kernel, [((24, ROW_COLS + LANES), f32), ((16, 3, 8, LANES), bf16)], scalars=1
    )(place, lines, embedding, ids, marks)
    got = total_and_relay(sent, "gz", ("gy", "gx"), 1)
    back = [((6, 6, EMBED, WIDE), bf16), ((4, 4, CHANNELS, WIDE), bf16)]
    block = ((3, 5, EMBED, LANES), bf16)
    mid, sent = kernel_call(kernels_kernel, [block, ((32, 4, 8, LANES), bf16)], scratch=back)(
        direct, got, wide, hidden, back_two
    )
    got = total_and_relay(sent, ("gy", "gx"), "gz", lax.axis_size("gx"))
    grad_features, grad_one, grad_bias, grad_two = kernel_call(
        last_kernel,
        [
            ((CHANNELS, 2, 2, LANES), bf16),
            ((27, CHANNELS, CHANNELS), f32),
            ((1, CHANNELS), f32),
            ((27, EMBED, CHANNELS), f32),
        ],
        scratch=[block, block] + back,
    )(got, mid, hidden, back_two, back_one)
    return (
        grad_features,
        grad_one.reshape(3, 3, 3, CHANNELS, CHANNELS),
        grad_bias.reshape(CHANNELS),
        grad_two.reshape(3, 3, 3, EMBED, CHANNELS),
    )


def solution(mesh):
    return jax.shard_map(
        shards,
        mesh=mesh,
        in_specs=(P(None, "gz", "gy", "gx"), P("gz", "gy", "gx"), P(), P(), P()),
        out_specs=(P(None, "gz", "gy", "gx"), P(), P(), P()),
        check_vma=False,
    )
```
